256 devices in a mesh: section: 8 (over x, y_lo), seq: 32 (over y_hi, z, core).
Axes of the slice: x: 4, y: 4 (y_hi: 2, y_lo: 2; y = y_hi * 2 + y_lo), z: 8, core: 2. Of those that a mesh axis runs over, the one named last changes fastest.
Arguments:
- acts: bfloat16 [8, 8, 2048, 1536], P('section', None, 'seq'), may hold values from -6 to 6
- attn_proj: bfloat16 [8, 4, 1536, 1536], P('section', None, 'seq'), may hold values from -0.15625 to 0.15625
- modulation: bfloat16 [8, 8, 3, 1536], P('section'), may hold values from -6 to 6
- q_gain: float32 [8, 1536], P('section'), may hold values from 0.8 to 72, as said below
- text_feat: bfloat16 [8, 256, 4096], P(None, 'seq', 'section'), may hold values from -6 to 6
- text_proj: bfloat16 [4096, 1536], P('section'), may hold values from -0.09375 to 0.09375
- text_len: int32 [8], replicated, may hold values from 64 to 256
- kv_index: int32 [16, 4], replicated, may hold values from 0 to 15, as said below
- kv_count: int32 [16], replicated, may hold values from 1 to 4
Outputs:
- received: bfloat16 [8, 8, 2048, 1536], P('section', None, 'seq')
The draws below stay inside these ranges and needn't reach their ends.
Inputs may be any that keep to these rules, and one draw needn't show every extreme that they name: `q_gain`: heads differ in scale; the gain is the same within a head up to a factor within 0.8 to 1.2 for each feature. `kv_index`: every row starts with its own tile; the first kv_count entries of a row are distinct; entries past kv_count repeat the row's own tile.
All inputs are finite; a program needn't handle non-finite values.
Results may differ from the reference program's by a relative error of at most 0.0075.
The reference program's roundings to bfloat16 on the way count: a program that leaves them out, or rounds other values in their place, can miss the bound.
Values may be sent and summed in bfloat16 or wider, within the bound.
No kernel may reach another device: no remote copies, remote signals or barrier semaphores. Data moves between devices by JAX's collectives and lax.ppermute only.
A program may use at most 128 MiB of HBM per device.

```python
import math
import jax
import jax.numpy as jnp
from jax import lax

D = 1536
HEADS = 12
HEAD_DIM = 128
DT = 4096
TXT = 256
SEQS = 8
KMAX = 4
LEN = 2048
NT = 16
N_SECTION = 8


def tile_lists(key):
    row_keys = jax.random.split(key, NT + 2)

    def shuffled(one_key):
        return jax.random.permutation(one_key, NT)
    ranks = jax.vmap(shuffled)(row_keys[:NT]).astype(jnp.int32)
    own = jnp.arange(NT, dtype=jnp.int32)
    ranks = jnp.where(own[None, :] == own[:, None], -1, ranks)
    order = jnp.argsort(ranks, axis=1, stable=True)[:, :KMAX].astype(jnp.int32)
    counts = jax.random.randint(row_keys[NT], (NT,), 1, KMAX + 1).astype(jnp.int32)
    chosen = jax.random.permutation(row_keys[NT + 1], NT)
    counts = counts.at[chosen[0]].set(KMAX)
    counts = counts.at[chosen[1]].set(1)
    slots = jnp.arange(KMAX, dtype=jnp.int32)
    lists = jnp.where(slots[None, :] < counts[:, None], order, own[:, None])
    return (lists.astype(jnp.int32), counts.astype(jnp.int32))


def draw_kv_index(key, part):
    lists, counts = tile_lists(key)
    return lists


def draw_kv_count(key, part):
    lists, counts = tile_lists(key)
    return counts


def draw_text_len(key, part):
    key = jax.random.fold_in(key, 5)
    lens = jax.random.randint(key, (SEQS,), TXT // 4, TXT + 1).astype(jnp.int32)
    chosen = jax.random.permutation(jax.random.fold_in(key, 1), SEQS)
    lens = lens.at[chosen[0]].set(TXT)
    lens = lens.at[chosen[1]].set(TXT // 4)
    return lens.astype(jnp.int32)


def head_gains(key, ceiling):
    first, second = jax.random.split(key)
    head = jnp.exp(jax.random.uniform(first, (N_SECTION, HEADS), jnp.float32, 0.0, math.log(ceiling)))
    channel = 1.0 + 0.2 * jax.random.uniform(second, (N_SECTION, D), jnp.float32, -1.0, 1.0)
    return jnp.repeat(head, HEAD_DIM, axis=1) * channel


def draw_q_gain(key, part):
    key = jax.random.fold_in(key, 9)
    gains = head_gains(key, 3.0)
    return gains.astype(jnp.float32)


def level_of(stream_key, shape, cuts, low, largest):
    def one(position, parts):
        draws = jax.random.uniform(jax.random.fold_in(jax.random.fold_in(stream_key, 6), position), (parts,), jnp.float32, low / len(cuts), largest / len(cuts))
        return jnp.repeat(jnp.exp(draws), shape[position] // parts).reshape((-1,) + (1,) * (len(shape) - position - 1))

    loudness = one(*cuts[0])
    for cut in cuts[1:]:
        loudness = loudness * one(*cut)
    return loudness


def scatter_about(own_key, extent, scale, bound, cuts=(), kind=jnp.bfloat16):
    entries = jax.random.normal(own_key, extent, jnp.float32) * scale
    if len(cuts) > 0:
        entries = level_of(own_key, extent, cuts, -0.22, 0.18) * entries
    return jnp.clip(entries, min=-bound, max=bound).astype(kind)


def setup_inputs(seed: int = 0) -> dict:
    splits = jax.random.split(jax.random.key(seed), 10)
    acts = scatter_about(splits[0], (N_SECTION, SEQS, LEN, D), 1.0, 6.0, ((0, 8), (2, 32)))
    attn_proj = scatter_about(splits[1], (N_SECTION, 4, D, D), D ** -0.5, 0.15625, ((0, 8), (2, 32)))
    modulation = scatter_about(splits[2], (N_SECTION, SEQS, 3, D), 1.5, 6.0, ((0, 8),))
    q_gain = draw_q_gain(jax.random.fold_in(splits[9], 71), 0)
    text_feat = scatter_about(splits[4], (SEQS, TXT, DT), 1.0, 6.0, ((1, 32), (2, 8)))
    text_proj = scatter_about(splits[5], (DT, D), DT ** -0.5, 0.09375, ((0, 8),))
    text_len = draw_text_len(jax.random.fold_in(splits[9], 71), 0)
    kv_index = draw_kv_index(jax.random.fold_in(splits[9], 71), 0)
    kv_count = draw_kv_count(jax.random.fold_in(splits[9], 71), 0)
    return {"acts": acts, "attn_proj": attn_proj, "modulation": modulation, "q_gain": q_gain, "text_feat": text_feat, "text_proj": text_proj, "text_len": text_len, "kv_index": kv_index, "kv_count": kv_count}


def unit_rows(values):
    return values * lax.rsqrt(lax.optimization_barrier(jnp.mean(values * values, axis=-1, keepdims=True)) + 1e-06)

def attend(query, keys, values, text_keys, text_values, text_count, kv_index, kv_count):
    length, head_dim = query.shape
    tiles, slots = kv_index.shape
    tile = length // tiles
    group = math.gcd(tiles, max(1, 512 // tile))
    key_tiles = keys.reshape(tiles, tile, head_dim).astype(jnp.float32)
    value_tiles = values.reshape(tiles, tile, head_dim).astype(jnp.float32)
    text_keys32 = text_keys.astype(jnp.float32)
    text_values32 = text_values.astype(jnp.float32)
    scale = 1.0 / math.sqrt(head_dim)
    text_valid = jnp.arange(text_keys.shape[0], dtype=jnp.int32) < text_count

    def block(start):
        lists = lax.dynamic_slice_in_dim(kv_index, start, group, 0)
        counts = lax.dynamic_slice_in_dim(kv_count, start, group, 0)
        rows = lax.dynamic_slice_in_dim(query, start * tile, group * tile, 0).reshape(group, tile, head_dim).astype(jnp.float32)
        near_keys = key_tiles[lists].reshape(group, slots * tile, head_dim)
        near_values = value_tiles[lists].reshape(group, slots * tile, head_dim)
        video_scores = jnp.einsum('gqe,gke->gqk', rows, near_keys) * scale
        text_scores = jnp.einsum('gqe,ke->gqk', rows, text_keys32) * scale
        live = jnp.repeat(jnp.arange(slots, dtype=jnp.int32)[None, :] < counts[:, None], tile, axis=1)
        video_scores = jnp.where(live[:, None, :], video_scores, -jnp.inf)
        text_scores = jnp.where(text_valid[None, None, :], text_scores, -jnp.inf)
        top = jnp.maximum(lax.optimization_barrier(jnp.max(video_scores, axis=-1)), lax.optimization_barrier(jnp.max(text_scores, axis=-1)))[..., None]
        video_exp = jnp.exp(video_scores - top)
        text_exp = jnp.exp(text_scores - top)
        denom = lax.optimization_barrier(jnp.sum(video_exp, axis=-1, keepdims=True)) + lax.optimization_barrier(jnp.sum(text_exp, axis=-1, keepdims=True))
        video_probs = (video_exp / denom).astype(jnp.bfloat16).astype(jnp.float32)
        text_probs = (text_exp / denom).astype(jnp.bfloat16).astype(jnp.float32)
        mixed = jnp.einsum('gqk,gke->gqe', video_probs, near_values) + jnp.einsum('gqk,ke->gqe', text_probs, text_values32)
        return mixed.astype(jnp.bfloat16)
    starts = jnp.arange(tiles // group, dtype=jnp.int32) * group
    return lax.map(block, starts).reshape(length, head_dim)

def layer(acts, weights, modulation, q_gain, text_emb, text_len, kv_index, kv_count):
    inputs = acts.astype(jnp.float32)
    mean = lax.optimization_barrier(jnp.mean(inputs, axis=-1, keepdims=True))
    variance = lax.optimization_barrier(jnp.mean((inputs - mean) ** 2, axis=-1, keepdims=True))
    shift = modulation[:, 0][:, None, :].astype(jnp.float32)
    scale = modulation[:, 1][:, None, :].astype(jnp.float32)
    gate = modulation[:, 2][:, None, :].astype(jnp.float32)
    modulated = ((inputs - mean) * lax.rsqrt(variance + 1e-06) * (1.0 + scale) + shift).astype(jnp.bfloat16)
    heads_w = weights[:3].reshape(3, D, HEADS, HEAD_DIM).astype(jnp.float32)
    projected = jnp.einsum('std,kdhe->kshte', modulated.astype(jnp.float32), heads_w)
    gain = q_gain.reshape(HEADS, HEAD_DIM)[None, :, None, :]
    query = (unit_rows(projected[0]) * gain).astype(jnp.bfloat16)
    keys = unit_rows(projected[1]).astype(jnp.bfloat16)
    values = projected[2].astype(jnp.bfloat16)
    text_in = jnp.einsum('std,kdhe->kshte', text_emb.astype(jnp.float32), heads_w[1:])
    text_keys = unit_rows(text_in[0]).astype(jnp.bfloat16)
    text_values = text_in[1].astype(jnp.bfloat16)
    slot_lens = jnp.repeat(text_len, HEADS)

    def one_slot(item):
        return attend(item[0], item[1], item[2], item[3], item[4], item[5], kv_index, kv_count)
    attended = lax.map(one_slot, (query.reshape(SEQS * HEADS, LEN, HEAD_DIM), keys.reshape(SEQS * HEADS, LEN, HEAD_DIM), values.reshape(SEQS * HEADS, LEN, HEAD_DIM), text_keys.reshape(SEQS * HEADS, TXT, HEAD_DIM), text_values.reshape(SEQS * HEADS, TXT, HEAD_DIM), slot_lens))
    by_token = attended.reshape(SEQS, HEADS, LEN, HEAD_DIM).transpose(0, 2, 1, 3).reshape(SEQS * LEN, D)
    output = jnp.dot(by_token, weights[3], preferred_element_type=jnp.float32).reshape(SEQS, LEN, D)
    return (inputs + gate * output).astype(jnp.bfloat16)

def reference(acts, attn_proj, modulation, q_gain, text_feat, text_proj, text_len, kv_index, kv_count):
    text_total = jnp.einsum('std,de->ste', text_feat.astype(jnp.float32), text_proj.astype(jnp.float32))
    text_emb = unit_rows(text_total).astype(jnp.bfloat16)
    results = []
    for section in range(N_SECTION):
        results.append(layer(acts[section], attn_proj[section], modulation[section], q_gain[section], text_emb, text_len, kv_index, kv_count))
    stacked = jnp.stack(results)
    return jnp.roll(stacked, 1, axis=0)
```

```python
import math

import jax
import jax.numpy as jnp
from jax import lax
from jax.experimental import pallas as pl
from jax.experimental.pallas import tpu as pltpu
from jax.sharding import Mesh
from jax.sharding import PartitionSpec as P

HEADS = 12
HEAD_DIM = 128
MEMBERS = 4
PER = HEADS // MEMBERS
COLS = PER * HEAD_DIM
SEQ = ("yh", "z", "core")
NEG = -1e30


def unit_rows(values):
    return values * lax.rsqrt(jnp.mean(values * values, axis=-1, keepdims=True) + 1e-06)


def project_kernel(place, m0, m1, m2, m3, w, gain, q, k, v, ws, xs):
    step = pl.program_id(0)
    rows = w.shape[3]
    width = ws.shape[0]

    @pl.when(step == 0)
    def _():
        for z in range(w.shape[0]):
            for member in range(MEMBERS):
                yh, core = member // 2, member % 2
                start = (yh * 16 + z * 2 + core) * rows
                for kind in range(3):
                    ws[start : start + rows, kind * COLS : (kind + 1) * COLS] = w[z, member, kind]

    for part, block in enumerate((m0, m1, m2, m3)):

        @pl.when(step // 2 == part)
        def _(block=block):
            xs[...] = block[...]

    for kind, out in enumerate((q, k, v)):
        made = jnp.dot(
            xs[...], ws[:, kind * COLS : (kind + 1) * COLS], preferred_element_type=jnp.float32
        )
        for head in range(PER):
            lanes = slice(head * HEAD_DIM, (head + 1) * HEAD_DIM)
            mine = made[:, lanes]
            if kind < 2:
                mine = unit_rows(mine)
            if kind == 0:
                mine = mine * gain[:, lanes]
            out[0, :, 0, :, lanes] = mine.astype(jnp.bfloat16).reshape(4, 64, HEAD_DIM)


def project(place, parts, w, gain):
    def part_map(part):
        return lambda i, place: (jnp.clip(i - 2 * part, 0, 1), 0)

    width = parts[0].shape[1]
    half = parts[0].shape[0] // 2
    out_block = pl.BlockSpec(
        (1, 4, 1, 64, COLS), lambda i, place: (i // 4, i % 2, (i // 2) % 2, 0, 0)
    )
    out = jax.ShapeDtypeStruct((2, 8, 2, 64, COLS), jnp.bfloat16)
    return pl.pallas_call(
        project_kernel,
        out_shape=(out, out, out, jax.ShapeDtypeStruct((width, 3 * COLS), jnp.bfloat16)),
        grid_spec=pltpu.PrefetchScalarGridSpec(
            num_scalar_prefetch=1,
            grid=(8,),
            in_specs=[pl.BlockSpec((half, width), part_map(part)) for part in range(4)]
            + [
                pl.BlockSpec(w.shape, lambda i, place: (0,) * 5),
                pl.BlockSpec(gain.shape, lambda i, place: (0, 0)),
            ],
            out_specs=[out_block] * 3
            + [pl.BlockSpec((width, 3 * COLS), lambda i, place: (0, 0))],
            scratch_shapes=[pltpu.VMEM((half, width), jnp.bfloat16)],
        ),
        compiler_params=pltpu.CompilerParams(vmem_limit_bytes=50 * 2**20),
        cost_estimate=pl.CostEstimate(
            flops=2 * 2048 * 1536 * 1152, bytes_accessed=18 * 2**20, transcendentals=0
        ),
        name="project",
    )(place, *parts, w, gain)


def attend_kernel(place, kv_index, kv_count, text_len, text, ws, q, k, v, out, tk, tv):
    yh, z, core = place[0], place[1], place[2]
    made = jnp.dot(text[...], ws[:, COLS:], preferred_element_type=jnp.float32)
    for head in range(PER):
        lanes = slice(head * HEAD_DIM, (head + 1) * HEAD_DIM)
        tk[:, lanes] = unit_rows(made[:, lanes]).astype(jnp.bfloat16)
        tv[:, lanes] = made[:, COLS + head * HEAD_DIM : COLS + (head + 1) * HEAD_DIM].astype(
            jnp.bfloat16
        )
    scale = 1.0 / math.sqrt(HEAD_DIM)
    tile = q.shape[1]
    txt = text.shape[0]
    valid = lax.broadcasted_iota(jnp.int32, (tile, txt), 1) < text_len[z]
    contract = (((1,), (1,)), ((), ()))

    def one_tile(i, carry):
        slot = lax.rem(i + 8 * yh, 16)
        count = kv_count[i]
        near = [lax.rem(kv_index[i, c] + 8 * yh, 16) for c in range(4)]
        for n in range(1, 5):

            @pl.when(count == n)
            def _(n=n):
                for head in range(PER):
                    lanes = slice(head * HEAD_DIM, (head + 1) * HEAD_DIM)
                    rows = q[slot, :, lanes]
                    scores = [
                        lax.dot_general(
                            rows, k[near[c], :, lanes], contract, preferred_element_type=jnp.float32
                        )
                        * scale
                        for c in range(n)
                    ]
                    text_scores = (
                        lax.dot_general(
                            rows, tk[:, lanes], contract, preferred_element_type=jnp.float32
                        )
                        * scale
                    )
                    scores.append(jnp.where(valid, text_scores, NEG))
                    top = jnp.max(scores[-1], axis=-1, keepdims=True)
                    for one in scores[:-1]:
                        top = jnp.maximum(top, jnp.max(one, axis=-1, keepdims=True))
                    exps = [jnp.exp(one - top) for one in scores]
                    denom = jnp.sum(exps[-1], axis=-1, keepdims=True)
                    for one in exps[:-1]:
                        denom = denom + jnp.sum(one, axis=-1, keepdims=True)
                    inverse = 1.0 / denom
                    probs = [(one * inverse).astype(jnp.bfloat16) for one in exps]
                    mixed = jnp.dot(probs[-1], tv[:, lanes], preferred_element_type=jnp.float32)
                    for c in range(n):
                        mixed = mixed + jnp.dot(
                            probs[c], v[near[c], :, lanes], preferred_element_type=jnp.float32
                        )
                    mixed = mixed.astype(jnp.bfloat16)
                    out[2 * i + core, :, lanes] = mixed[: tile // 2]
                    out[2 * i + 1 - core, :, lanes] = mixed[tile // 2 :]

        return carry

    lax.fori_loop(0, 16, one_tile, 0)


def attend(place, kv_index, kv_count, text_len, text, ws, q, k, v):
    smem = pl.BlockSpec(memory_space=pltpu.SMEM)
    vmem = pl.BlockSpec(memory_space=pltpu.VMEM)
    return pl.pallas_call(
        attend_kernel,
        out_shape=jax.ShapeDtypeStruct((32, 64, COLS), jnp.bfloat16),
        in_specs=[smem] * 4 + [vmem] * 5,
        out_specs=vmem,
        scratch_shapes=[
            pltpu.VMEM((text.shape[0], COLS), jnp.bfloat16),
            pltpu.VMEM((text.shape[0], COLS), jnp.bfloat16),
        ],
        compiler_params=pltpu.CompilerParams(vmem_limit_bytes=40 * 2**20),
        cost_estimate=pl.CostEstimate(
            flops=3 * 10**9, bytes_accessed=11 * 2**20, transcendentals=5 * 10**6
        ),
        name="attend",
    )(place, kv_index, kv_count, text_len, text, ws, q, k, v)


def finish_kernel(att, wo, acts, gate, out, xs):
    for one in range(2):
        for member in range(MEMBERS):
            xs[one * 64 : (one + 1) * 64, member * COLS : (member + 1) * COLS] = att[
                member // 2, one, member % 2
            ]
    made = jnp.dot(xs[...], wo[...], preferred_element_type=jnp.float32)
    for one in range(2):
        out[one] = (
            acts[one].astype(jnp.float32)
            + gate[one].astype(jnp.float32) * made[one * 64 : (one + 1) * 64]
        ).astype(jnp.bfloat16)


def finish(att, wo, acts, gate):
    width = acts.shape[2]
    rows = pl.BlockSpec((2, 64, width), lambda i: (i, 0, 0))
    return pl.pallas_call(
        finish_kernel,
        grid=(4,),
        out_shape=jax.ShapeDtypeStruct(acts.shape, jnp.bfloat16),
        in_specs=[
            pl.BlockSpec((2, 2, 2, 64, COLS), lambda i: (0, i, 0, 0, 0)),
            pl.BlockSpec(wo.shape, lambda i: (0, 0)),
            rows,
            pl.BlockSpec((2, 1, width), lambda i: (i, 0, 0)),
        ],
        out_specs=rows,
        scratch_shapes=[pltpu.VMEM((128, width), jnp.bfloat16)],
        compiler_params=pltpu.CompilerParams(vmem_limit_bytes=40 * 2**20),
        cost_estimate=pl.CostEstimate(
            flops=2 * 512 * 1536 * 1536, bytes_accessed=10 * 2**20, transcendentals=0
        ),
        name="finish",
    )(att, wo, acts, gate)


def swap(block, axis):
    return lax.ppermute(block, axis, [(0, 1), (1, 0)])


def body(acts, attn_proj, modulation, q_gain, text_feat, text_proj, text_len, kv_index, kv_count):
    acts, weights, modulation = acts[0], attn_proj[0], modulation[0]
    width = acts.shape[2]
    yh, z, core = (lax.axis_index(name) for name in SEQ)
    member = 2 * yh + core
    place = jnp.stack([yh, z, core]).astype(jnp.int32)

    inputs = acts.astype(jnp.float32)
    mean = jnp.mean(inputs, axis=-1, keepdims=True)
    variance = jnp.mean((inputs - mean) ** 2, axis=-1, keepdims=True)
    shift = modulation[:, 0][:, None, :].astype(jnp.float32)
    scale = modulation[:, 1][:, None, :].astype(jnp.float32)
    modulated = ((inputs - mean) * lax.rsqrt(variance + 1e-06) * (1.0 + scale) + shift).astype(
        jnp.bfloat16
    )
    own = lax.all_to_all(modulated, "z", split_axis=0, concat_axis=0, tiled=True)

    inner = weights[:3].reshape(3, weights.shape[1], MEMBERS, COLS).transpose(2, 0, 1, 3)
    inner = lax.all_to_all(inner, ("yh", "core"), split_axis=0, concat_axis=0, tiled=True)
    inner = lax.all_gather(inner, "z", axis=0)

    part = jnp.dot(
        text_feat.reshape(-1, text_feat.shape[2]), text_proj, preferred_element_type=jnp.float32
    ).reshape(text_feat.shape[0], text_feat.shape[1], width)
    part = lax.all_to_all(part, "section", split_axis=0, concat_axis=0, tiled=True)
    text = unit_rows(jnp.sum(part, axis=0)).astype(jnp.bfloat16)
    text = lax.all_gather(text, SEQ, axis=0, tiled=True)
    route = []
    for s in range(8):
        for y in range(2):
            for zz in range(8):
                for c in range(2):
                    route.append((((s * 2 + y) * 8 + zz) * 2 + c, ((zz * 2 + y) * 8 + s) * 2 + c))
    text = lax.ppermute(text, ("section",) + SEQ, route)

    own = own.reshape(-1, width)
    across = swap(own, "yh")
    near = swap(own, "core")
    far = swap(across, "core")
    gain = lax.dynamic_slice_in_dim(q_gain, member * COLS, COLS, 1)
    q, k, v, ws = project(place, (own, near, across, far), inner, gain)

    outer, inner = lax.optimization_barrier((weights[3], inner))
    outer = lax.all_gather(outer, SEQ, axis=0, tiled=True)

    tiles = (16, 128, COLS)
    attended = attend(
        place,
        kv_index,
        kv_count,
        text_len,
        text,
        ws,
        q.reshape(tiles),
        k.reshape(tiles),
        v.reshape(tiles),
    )
    attended = lax.all_to_all(attended, SEQ, split_axis=0, concat_axis=0, tiled=True)
    gate = modulation[:, 2][:, None, :]
    fresh = finish(attended.reshape(2, 8, 2, 64, COLS), outer, acts, gate)
    return lax.ppermute(fresh[None], "section", [(i, (i + 1) % 8) for i in range(8)])


def solution(mesh):
    fine = Mesh(mesh.devices.reshape(8, 2, 8, 2), ("section",) + SEQ)
    in_specs = (
        P("section", None, SEQ, None),
        P("section", None, SEQ, None),
        P("section", None, None, None),
        P("section", None),
        P(None, SEQ, "section"),
        P("section", None),
        P(),
        P(),
        P(),
    )
    out_specs = P("section", None, SEQ, None)
    return jax.shard_map(body, mesh=fine, in_specs=in_specs, out_specs=out_specs, check_vma=False)
```

```python
import math

import jax
import jax.numpy as jnp
from jax import lax
from jax.experimental import pallas as pl
from jax.experimental.pallas import tpu as pltpu
from jax.sharding import Mesh
from jax.sharding import PartitionSpec as P

HEADS = 12
HEAD_DIM = 128
MEMBERS = 4
PER = HEADS // MEMBERS
COLS = PER * HEAD_DIM
SECTIONS = 8
RING = 8
SEQ = ("yh", "z", "core")
NEG = -1e30
VMEM = pl.BlockSpec(memory_space=pltpu.VMEM)
SMEM = pl.BlockSpec(memory_space=pltpu.SMEM)
FAR = (4, 3, 5, 2)
NEAR = (6, 1, 7, 0)
RING_ORDER = (0, -1, 1, -2, 2, -3, 3, 4)


def unit_rows(values):
    return values * lax.rsqrt(jnp.mean(values * values, axis=-1, keepdims=True) + 1e-06)


def flip(bit, other):
    return bit + other - 2 * bit * other


def project_kernel(place, m0, m1, m2, m3, *refs):
    w0, wr1, wl1, wr2, wl2, wr3, wl3, wr4, wl4, gain, q, k, v, ws, xs = refs
    step = pl.program_id(0)
    rows = w0.shape[1]
    yh, z, core = place[0], place[1], place[2]

    @pl.when(step == 0)
    def _():
        def lay(block, first, count, offset):
            source = lax.rem(z + offset + RING, RING)
            for at in range(first, first + count):
                member, kind = at // 3, at % 3
                source_yh = flip(yh, member // 2)
                source_core = flip(core, member % 2)
                start = pl.multiple_of((source_yh * 16 + source * 2 + source_core) * rows, 16)
                ws[pl.ds(start, rows), kind * COLS : (kind + 1) * COLS] = block[at - first]

        for block, offset in (
            (w0, 0), (wr1, -1), (wl1, 1), (wr2, -2), (wl2, 2), (wr3, -3), (wl3, 3)
        ):
            lay(block, 0, 12, offset)
        lay(wr4, 0, 8, 4)
        lay(wl4, 8, 4, 4)

    for part, block in enumerate((m0, m1, m2, m3)):

        @pl.when(step == part)
        def _(block=block):
            xs[...] = block[...]

    made = jnp.dot(xs[...], ws[...], preferred_element_type=jnp.float32)
    for kind, out in enumerate((q, k, v)):
        for head in range(PER):
            lanes = slice(head * HEAD_DIM, (head + 1) * HEAD_DIM)
            first = kind * COLS + head * HEAD_DIM
            mine = made[:, first : first + HEAD_DIM]
            if kind < 2:
                mine = unit_rows(mine)
            if kind == 0:
                mine = mine * gain[:, lanes]
            out[0, :, 0, :, lanes] = mine.astype(jnp.bfloat16).reshape(8, 64, HEAD_DIM)


def project(place, parts, blocks, gain):
    rows, width = parts[0].shape

    def whole(array):
        return pl.BlockSpec(
            array.shape, lambda i, place: (0,) * array.ndim, pipeline_mode=pl.Buffered(1)
        )

    out_block = pl.BlockSpec((1, 8, 1, 64, COLS), lambda i, place: (i // 2, 0, i % 2, 0, 0))
    out = jax.ShapeDtypeStruct((2, 8, 2, 64, COLS), jnp.bfloat16)
    return pl.pallas_call(
        project_kernel,
        out_shape=(out, out, out, jax.ShapeDtypeStruct((width, 3 * COLS), jnp.bfloat16)),
        grid_spec=pltpu.PrefetchScalarGridSpec(
            num_scalar_prefetch=1,
            grid=(4,),
            in_specs=[whole(array) for array in (*parts, *blocks, gain)],
            out_specs=[out_block] * 3
            + [pl.BlockSpec((width, 3 * COLS), lambda i, place: (0, 0))],
            scratch_shapes=[pltpu.VMEM((rows, width), jnp.bfloat16)],
        ),
        compiler_params=pltpu.CompilerParams(vmem_limit_bytes=50 * 2**20),
        cost_estimate=pl.CostEstimate(
            flops=2 * 2048 * 1536 * 1152, bytes_accessed=18 * 2**20, transcendentals=0
        ),
        name="project",
    )(place, *parts, *blocks, gain)


def text_kernel(t0, t1, t2, t3, ws, tk, tv, xs):
    for part, block in enumerate((t0, t1, t2, t3)):
        xs[part * 64 : (part + 1) * 64, :] = block[...]
    made = jnp.dot(xs[...], ws[:, COLS:], preferred_element_type=jnp.float32)
    for head in range(PER):
        lanes = slice(head * HEAD_DIM, (head + 1) * HEAD_DIM)
        tk[:, lanes] = unit_rows(made[:, lanes]).astype(jnp.bfloat16)
    tv[...] = made[:, COLS:].astype(jnp.bfloat16)


def text_pair(parts, ws):
    rows = 4 * parts[0].shape[0]
    out = jax.ShapeDtypeStruct((rows, COLS), jnp.bfloat16)
    return pl.pallas_call(
        text_kernel,
        out_shape=(out, out),
        in_specs=[VMEM] * 5,
        out_specs=(VMEM, VMEM),
        scratch_shapes=[pltpu.VMEM((rows, parts[0].shape[1]), jnp.bfloat16)],
        compiler_params=pltpu.CompilerParams(vmem_limit_bytes=30 * 2**20),
        cost_estimate=pl.CostEstimate(
            flops=2 * 256 * 1536 * 768, bytes_accessed=5 * 2**20, transcendentals=0
        ),
        name="text_pair",
    )(*parts, ws)


def attend(distances, place, kv_index, kv_count, text_len, tk, tv, q, k, v):
    tile = q.shape[1]
    txt = tk.shape[0]

    def kernel(place, kv_index, kv_count, text_len, tk, tv, q, k, v, o0, o1, o2, o3, kc, vc):
        yh, z, core = place[0], place[1], place[2]
        kc[:txt, :] = tk[...]
        vc[:txt, :] = tv[...]
        scale = 1.0 / math.sqrt(HEAD_DIM)
        row = lax.broadcasted_iota(jnp.int32, (tile, txt), 1)
        row_yh = flip(row // 128, yh)
        row_core = flip((row // 64) % 2, core)
        token = (row_yh * 16 + ((row // 8) % 8) * 2 + row_core) * 8 + row % 8
        valid = token < text_len[z]
        contract = (((1,), (1,)), ((), ()))
        for distance, out in zip(distances, (o0, o1, o2, o3)):

            def one_tile(ry, carry, distance=distance, out=out):
                home = lax.rem(z + distance, RING)
                slot = ry * 8 + home
                index = flip(yh, ry) * 8 + home
                count = kv_count[index]
                for c in range(4):
                    near = lax.rem(kv_index[index, c] + 8 * yh, 16)
                    here = slice(txt + c * tile, txt + (c + 1) * tile)
                    kc[here, :] = k[near]
                    vc[here, :] = v[near]
                for n in range(1, 5):

                    @pl.when(count == n)
                    def _(n=n):
                        size = txt + n * tile
                        for head in range(PER):
                            lanes = slice(head * HEAD_DIM, (head + 1) * HEAD_DIM)
                            scores = (
                                lax.dot_general(
                                    q[slot, :, lanes],
                                    kc[:size, lanes],
                                    contract,
                                    preferred_element_type=jnp.float32,
                                )
                                * scale
                            )
                            scores = jnp.concatenate(
                                [jnp.where(valid, scores[:, :txt], NEG), scores[:, txt:]], axis=1
                            )
                            top = jnp.max(scores, axis=-1, keepdims=True)
                            exps = jnp.exp(scores - top)
                            inverse = 1.0 / jnp.sum(exps, axis=-1, keepdims=True)
                            probs = (exps * inverse).astype(jnp.bfloat16)
                            mixed = jnp.dot(
                                probs, vc[:size, lanes], preferred_element_type=jnp.float32
                            ).astype(jnp.bfloat16)
                            out[2 * ry, :, lanes] = mixed[: tile // 2]
                            out[2 * ry + 1, :, lanes] = mixed[tile // 2 :]

                return carry

            lax.fori_loop(0, 2, one_tile, 0)

    out = jax.ShapeDtypeStruct((MEMBERS, tile // 2, COLS), jnp.bfloat16)
    return pl.pallas_call(
        kernel,
        out_shape=(out,) * 4,
        in_specs=[SMEM] * 4 + [VMEM] * 5,
        out_specs=(VMEM,) * 4,
        scratch_shapes=[
            pltpu.VMEM((txt + 4 * tile, COLS), jnp.bfloat16),
            pltpu.VMEM((txt + 4 * tile, COLS), jnp.bfloat16),
        ],
        compiler_params=pltpu.CompilerParams(vmem_limit_bytes=30 * 2**20),
        cost_estimate=pl.CostEstimate(
            flops=3 * 10**9, bytes_accessed=6 * 2**20, transcendentals=3 * 10**6
        ),
        name="attend",
    )(place, kv_index, kv_count, text_len, tk, tv, q, k, v)


def finish_kernel(place, *refs):
    own, others = refs[:8], refs[8:14]
    pieces, (acts, gate, out, ws, xs) = refs[14:18], refs[18:]
    yh, z, core = place[0], place[1], place[2]
    rows = pieces[0].shape[2]
    for slot, offset in enumerate(RING_ORDER):
        source = lax.rem(z + offset + RING, RING)
        for other, block in enumerate(pieces):
            source_yh = flip(yh, other // 2)
            source_core = flip(core, other % 2)
            start = pl.multiple_of((source_yh * 16 + source * 2 + source_core) * rows, 16)
            for group in range(4):
                ws[pl.ds(start, rows), group * COLS : (group + 1) * COLS] = block[slot, group]
    for at in range(8):
        here = slice(at * 64, (at + 1) * 64)
        xs[0, here, :] = own[at][0]
        for other in range(3):
            xs[other + 1, here, :] = others[(at // 4) * 3 + other][at % 4]
    made = None
    for other in range(MEMBERS):
        heads = flip(yh, other // 2) * 2 + flip(core, other % 2)
        start = pl.multiple_of(heads * COLS, 128)
        term = jnp.dot(xs[other], ws[pl.ds(start, COLS), :], preferred_element_type=jnp.float32)
        made = term if made is None else made + term
    for at, distance in enumerate(FAR + NEAR):
        sequence = lax.rem(z - distance + RING, RING)
        start = pl.multiple_of(sequence * 64, 64)
        out[sequence] = (
            acts[pl.ds(start, 64), :].astype(jnp.float32)
            + gate[sequence] * made[at * 64 : (at + 1) * 64]
        ).astype(jnp.bfloat16)


def finish(place, own, others, pieces, acts, gate):
    width = acts.shape[1]
    return pl.pallas_call(
        finish_kernel,
        out_shape=jax.ShapeDtypeStruct((8, 64, width), jnp.bfloat16),
        in_specs=[SMEM] + [VMEM] * 20,
        out_specs=VMEM,
        scratch_shapes=[
            pltpu.VMEM((width, width), jnp.bfloat16),
            pltpu.VMEM((MEMBERS, 512, COLS), jnp.bfloat16),
        ],
        compiler_params=pltpu.CompilerParams(vmem_limit_bytes=50 * 2**20),
        cost_estimate=pl.CostEstimate(
            flops=2 * 512 * 1536 * 1536, bytes_accessed=12 * 2**20, transcendentals=0
        ),
        name="finish",
    )(place, *own, *others, *pieces, acts, gate)


def swap(block, axis):
    return lax.ppermute(block, axis, [(0, 1), (1, 0)])


def toggled(block, axis, bits, size):
    return lax.ppermute(block, axis, [(i, i ^ bits) for i in range(size)])


def moved(block, distance):
    return lax.ppermute(block, "z", [(i, (i + distance) % RING) for i in range(RING)])


def after(block, *earlier):
    for one in earlier:
        block = block + (one[(0,) * one.ndim] * 0).astype(block.dtype)
    return block


def text_rows(text_feat, text_proj):
    section = lax.axis_index("section")
    width = text_proj.shape[1]
    part = jnp.dot(
        text_feat.reshape(-1, text_feat.shape[2]), text_proj, preferred_element_type=jnp.float32
    ).reshape(2, 2, 2, -1, width)
    bits = [(section >> n) & 1 for n in range(3)]
    for n in range(3):
        keep = lax.dynamic_index_in_dim(part, bits[n], 2 - n, keepdims=False)
        send = lax.dynamic_index_in_dim(part, 1 - bits[n], 2 - n, keepdims=False)
        part = keep + toggled(send, "section", 1 << n, SECTIONS)
    rows = unit_rows(part).astype(jnp.bfloat16)
    for n in (2, 1, 0):
        rows = jnp.stack([rows, toggled(rows, "section", 1 << n, SECTIONS)], axis=2 - n)
    for n in range(3):
        rows = jnp.where(bits[n] == 1, jnp.flip(rows, 2 - n), rows)
    return rows.reshape(SECTIONS, -1, width)


def body(acts, attn_proj, modulation, q_gain, text_feat, text_proj, text_len, kv_index, kv_count):
    acts, weights, modulation = acts[0], attn_proj[0], modulation[0]
    sequences, tokens, width = acts.shape
    yh, z, core = (lax.axis_index(name) for name in SEQ)
    member = 2 * yh + core
    place = jnp.stack([yh, z, core]).astype(jnp.int32)

    inputs = acts.astype(jnp.float32)
    mean = jnp.mean(inputs, axis=-1, keepdims=True)
    variance = jnp.mean((inputs - mean) ** 2, axis=-1, keepdims=True)
    shift = modulation[:, 0][:, None, :].astype(jnp.float32)
    scale = modulation[:, 1][:, None, :].astype(jnp.float32)
    modulated = ((inputs - mean) * lax.rsqrt(variance + 1e-06) * (1.0 + scale) + shift).astype(
        jnp.bfloat16
    )
    own = lax.all_to_all(modulated, "z", split_axis=0, concat_axis=0, tiled=True)
    own = own.reshape(-1, width)

    packed = jnp.concatenate([acts.reshape(-1, width), modulation[:, 2], weights[3]])
    packed = lax.ppermute(packed, "section", [(i, (i + 1) % SECTIONS) for i in range(SECTIONS)])
    rows = sequences * tokens
    gate = packed[rows : rows + sequences].astype(jnp.float32)[:, None, :]
    outer = packed[rows + sequences :]

    mine = []
    for other in range(MEMBERS):
        columns = lax.dynamic_slice_in_dim(
            weights[:3], jnp.bitwise_xor(member, other) * COLS, COLS, 2
        )
        mine.append(toggled(columns, ("yh", "core"), other, MEMBERS) if other else columns)
    mine = jnp.concatenate([*mine, outer.reshape(-1, MEMBERS, COLS).transpose(1, 0, 2)])

    text_home = text_rows(text_feat, text_proj)

    near = swap(own, "core")
    across = swap(after(own, packed), "yh")
    far = swap(across, "core")
    right = left = after(mine, own)
    blocks = [right]
    for _ in range(3):
        right, left = moved(right, 1), moved(left, -1)
        blocks += [right, left]
    right, left = moved(right[:8], 1), moved(left[8:], -1)
    pieces = jnp.stack([one[12:] for one in blocks] + [left[4:]])
    pieces_across = swap(pieces, "yh")
    pieces = (pieces, swap(pieces, "core"), pieces_across, swap(pieces_across, "core"))
    text = lax.all_to_all(text_home, "z", split_axis=0, concat_axis=0, tiled=True)
    text = text.reshape(-1, width)
    text_across = swap(text, "yh")
    text_near = swap(text, "core")
    text_far = swap(text_across, "core")

    gain = lax.dynamic_slice_in_dim(q_gain, member * COLS, COLS, 1)
    q, k, v, ws = project(place, (own, near, across, far), (*blocks, right, left), gain)
    tk, tv = text_pair((text, text_near, text_across, text_far), ws)

    tiles = (16, 2 * tokens, COLS)
    shape = (tk, tv, q.reshape(tiles), k.reshape(tiles), v.reshape(tiles))
    far_made = attend(FAR, place, kv_index, kv_count, text_len, *shape)
    place_near = after(place, far_made[0])
    near_made = attend(NEAR, place_near, kv_index, kv_count, text_len, *shape)
    own_heads, other_heads = [], []
    for distance, block in zip(FAR + NEAR, far_made + near_made):
        route = [
            (s * RING + i, (s + 1) % SECTIONS * RING + (i + distance) % RING)
            for s in range(SECTIONS)
            for i in range(RING)
        ]
        own_heads.append(lax.ppermute(block, ("section", "z"), route))
    for half in range(2):
        for other in range(1, MEMBERS):
            block = jnp.stack([one[other] for one in own_heads[half * 4 : half * 4 + 4]])
            if half == 0:
                block = after(block, near_made[0])
            other_heads.append(toggled(block, ("yh", "core"), other, MEMBERS))
    fresh = finish(place, own_heads, other_heads, pieces, packed, gate)
    return fresh[None]


def solution(mesh):
    fine = Mesh(mesh.devices.reshape(SECTIONS, 2, RING, 2), ("section",) + SEQ)
    in_specs = (
        P("section", None, SEQ, None),
        P("section", None, SEQ, None),
        P("section", None, None, None),
        P("section", None),
        P(None, SEQ, "section"),
        P("section", None),
        P(),
        P(),
        P(),
    )
    out_specs = P("section", None, SEQ, None)
    return jax.shard_map(body, mesh=fine, in_specs=in_specs, out_specs=out_specs, check_vma=False)
```

```python
import math

import jax
import jax.numpy as jnp
from jax import lax
from jax.experimental import pallas as pl
from jax.experimental.pallas import tpu as pltpu
from jax.sharding import Mesh
from jax.sharding import PartitionSpec as P

HEADS = 12
HEAD_DIM = 128
MEMBERS = 4
PER = HEADS // MEMBERS
COLS = PER * HEAD_DIM
SECTIONS = 8
RING = 8
SEQ = ("yh", "z", "core")
NEG = -1e30
VMEM = pl.BlockSpec(memory_space=pltpu.VMEM)
SMEM = pl.BlockSpec(memory_space=pltpu.SMEM)
ORDER = (4, 3, 5, 2, 6, 1, 7, 0)
RING_ORDER = (0, -1, 1, -2, 2, -3, 3, 4)


def unit_rows(values):
    return values * lax.rsqrt(jnp.mean(values * values, axis=-1, keepdims=True) + 1e-06)


def flip(bit, other):
    return bit + other - 2 * bit * other


def layer_kernel(place, kv_index, kv_count, text_len, *refs):
    parts, blocks, texts, gain, refs = refs[:4], refs[4:13], refs[13:17], refs[17], refs[18:]
    outs, refs = refs[:8], refs[8:]
    xs, ws, ts, q, k, v, kc, vc, made, res, w_sem, t_sem, x_sem, out_sem = refs
    yh, z, core = place[0], place[1], place[2]
    rows = blocks[0].shape[1]
    tile, txt = q.shape[1], ts.shape[0]

    def lay(block, members, offset):
        source = lax.rem(z + offset + RING, RING)
        for at, member in enumerate(members):
            source_yh = flip(yh, member // 2)
            source_core = flip(core, member % 2)
            start = pl.multiple_of((source_yh * 16 + source * 2 + source_core) * rows, 16)
            pltpu.make_async_copy(block.at[at], ws.at[pl.ds(start, rows)], w_sem).start()

    for block, offset in zip(blocks[:7], RING_ORDER):
        lay(block, range(4), offset)
    lay(blocks[7], (0, 1), 4)
    lay(blocks[8], (2, 3), 4)
    loads = [pltpu.make_async_copy(one, xs.at[at], x_sem.at[at]) for at, one in enumerate(parts)]
    for load in loads:
        load.start()
    quarter = txt // 4
    text_loads = [
        pltpu.make_async_copy(one, ts.at[at * quarter : (at + 1) * quarter], t_sem.at[at])
        for at, one in enumerate(texts)
    ]
    for load in text_loads:
        load.start()
    pltpu.make_async_copy(ws, ws, w_sem).wait()

    def one_part(part, carry):
        for at, load in enumerate(loads):

            @pl.when(part == at)
            def _(load=load):
                load.wait()

        made[...] = jnp.dot(xs[part], ws[...], preferred_element_type=jnp.float32)
        slots = pl.ds(part // 2 * 8, 8)
        half = pl.ds(pl.multiple_of(part % 2 * (tile // 2), tile // 2), tile // 2)
        for kind, out in enumerate((q, k, v)):
            for head in range(PER):
                lanes = slice(head * HEAD_DIM, (head + 1) * HEAD_DIM)
                first = kind * COLS + head * HEAD_DIM
                mine = made[:, first : first + HEAD_DIM]
                if kind < 2:
                    mine = unit_rows(mine)
                if kind == 0:
                    mine = mine * gain[:, lanes]
                out[slots, half, lanes] = mine.astype(jnp.bfloat16).reshape(
                    8, tile // 2, HEAD_DIM
                )
        return carry

    lax.fori_loop(0, 4, one_part, 0)
    for load in text_loads:
        load.wait()
    pair = jnp.dot(ts[...], ws[:, COLS:], preferred_element_type=jnp.float32)
    for head in range(PER):
        lanes = slice(head * HEAD_DIM, (head + 1) * HEAD_DIM)
        kc[:txt, lanes] = unit_rows(pair[:, lanes]).astype(jnp.bfloat16)
    vc[:txt, :] = pair[:, COLS:].astype(jnp.bfloat16)

    scale = math.log2(math.e) / math.sqrt(HEAD_DIM)
    row = lax.broadcasted_iota(jnp.int32, (1, txt), 1)
    row_yh = flip(row // 128, yh)
    row_core = flip((row // 64) % 2, core)
    token = (row_yh * 16 + ((row // 8) % 8) * 2 + row_core) * 8 + row % 8
    bias = jnp.where(token < text_len[z], 0.0, NEG)
    contract = (((1,), (1,)), ((), ()))
    sends = [
        pltpu.make_async_copy(res.at[at], out, out_sem.at[at]) for at, out in enumerate(outs)
    ]

    def one_tile(step, carry):
        at, ry = step // 2, step % 2
        home = lax.rem(z + place[3 + at], RING)
        slot = ry * 8 + home
        index = flip(yh, ry) * 8 + home
        count = kv_count[index]
        for c in range(4):

            @pl.when(c < count)
            def _(c=c):
                near = lax.rem(kv_index[index, c] + 8 * yh, 16)
                here = slice(txt + c * tile, txt + (c + 1) * tile)
                kc[here, :] = k[near]
                vc[here, :] = v[near]

        for n in range(1, 5):

            @pl.when(count == n)
            def _(n=n):
                size = txt + n * tile
                for head in range(PER):
                    lanes = slice(head * HEAD_DIM, (head + 1) * HEAD_DIM)
                    scores = (
                        lax.dot_general(
                            q[slot, :, lanes],
                            kc[:size, lanes],
                            contract,
                            preferred_element_type=jnp.float32,
                        )
                        * scale
                    )
                    scores = jnp.concatenate([scores[:, :txt] + bias, scores[:, txt:]], axis=1)
                    top = jnp.max(scores, axis=-1, keepdims=True)
                    exps = jnp.exp2(scores - top)
                    inverse = 1.0 / jnp.sum(exps, axis=-1, keepdims=True)
                    probs = (exps * inverse).astype(jnp.bfloat16)
                    mixed = jnp.dot(
                        probs, vc[:size, lanes], preferred_element_type=jnp.float32
                    ).astype(jnp.bfloat16)
                    res[at, 2 * ry, :, lanes] = mixed[: tile // 2]
                    res[at, 2 * ry + 1, :, lanes] = mixed[tile // 2 :]

        for which, send in enumerate(sends):

            @pl.when(step == 2 * which + 1)
            def _(send=send):
                send.start()

        return carry

    lax.fori_loop(0, 16, one_tile, 0)
    for send in sends:
        send.wait()


def layer(place, kv_index, kv_count, text_len, parts, blocks, texts, gain):
    rows, width = parts[0].shape
    txt = 4 * texts[0].shape[0]
    tile = 128
    hbm = pl.BlockSpec(memory_space=pl.ANY)
    order = jnp.array(ORDER, jnp.int32)
    out = jax.ShapeDtypeStruct((MEMBERS, tile // 2, COLS), jnp.bfloat16)
    heads = pltpu.VMEM((16, tile, COLS), jnp.bfloat16)
    near = pltpu.VMEM((txt + 4 * tile, COLS), jnp.bfloat16)
    return pl.pallas_call(
        layer_kernel,
        out_shape=(out,) * 8,
        in_specs=[SMEM] * 4 + [hbm] * 17 + [VMEM],
        out_specs=(hbm,) * 8,
        scratch_shapes=[
            pltpu.VMEM((4, rows, width), jnp.bfloat16),
            pltpu.VMEM((width, 3 * COLS), jnp.bfloat16),
            pltpu.VMEM((txt, width), jnp.bfloat16),
            heads,
            heads,
            heads,
            near,
            near,
            pltpu.VMEM((rows, 3 * COLS), jnp.float32),
            pltpu.VMEM((8, MEMBERS, tile // 2, COLS), jnp.bfloat16),
            pltpu.SemaphoreType.DMA,
            pltpu.SemaphoreType.DMA((4,)),
            pltpu.SemaphoreType.DMA((4,)),
            pltpu.SemaphoreType.DMA((8,)),
        ],
        compiler_params=pltpu.CompilerParams(vmem_limit_bytes=48 * 2**20),
        cost_estimate=pl.CostEstimate(
            flops=12 * 10**9, bytes_accessed=14 * 2**20, transcendentals=5 * 10**6
        ),
        name="layer",
    )(jnp.concatenate([place, order]), kv_index, kv_count, text_len, *parts, *blocks, *texts, gain)


def finish_kernel(place, *refs):
    own, others = refs[:8], refs[8:14]
    wo, acts, gate, out, xs = refs[14:]
    yh, z, core = place[0], place[1], place[2]
    for at in range(8):
        here = slice(at * 64, (at + 1) * 64)
        xs[0, here, :] = own[at][0]
        for other in range(3):
            xs[other + 1, here, :] = others[(at // 4) * 3 + other][at % 4]
    made = None
    for other in range(MEMBERS):
        heads = flip(yh, other // 2) * 2 + flip(core, other % 2)
        start = pl.multiple_of(heads * COLS, 128)
        term = jnp.dot(xs[other], wo[pl.ds(start, COLS), :], preferred_element_type=jnp.float32)
        made = term if made is None else made + term
    for at, distance in enumerate(ORDER):
        sequence = lax.rem(z - distance + RING, RING)
        out[sequence] = (
            acts[sequence].astype(jnp.float32)
            + gate[sequence] * made[at * 64 : (at + 1) * 64]
        ).astype(jnp.bfloat16)


def finish(place, own, others, wo, acts, gate):
    return pl.pallas_call(
        finish_kernel,
        out_shape=jax.ShapeDtypeStruct(acts.shape, jnp.bfloat16),
        in_specs=[SMEM] + [VMEM] * 17,
        out_specs=VMEM,
        scratch_shapes=[
            pltpu.VMEM((MEMBERS, 512, COLS), jnp.bfloat16),
        ],
        compiler_params=pltpu.CompilerParams(vmem_limit_bytes=50 * 2**20),
        cost_estimate=pl.CostEstimate(
            flops=2 * 512 * 1536 * 1536, bytes_accessed=12 * 2**20, transcendentals=0
        ),
        name="finish",
    )(place, *own, *others, wo, acts, gate)


def swap(block, axis):
    return lax.ppermute(block, axis, [(0, 1), (1, 0)])


def toggled(block, axis, bits, size):
    return lax.ppermute(block, axis, [(i, i ^ bits) for i in range(size)])


def moved(block, distance):
    return lax.ppermute(block, "z", [(i, (i + distance) % RING) for i in range(RING)])


def after(block, *earlier):
    for one in earlier:
        block = block + (one[(0,) * one.ndim] * 0).astype(block.dtype)
    return block


def text_rows(text_feat, text_proj):
    section = lax.axis_index("section")
    width = text_proj.shape[1]
    part = jnp.dot(
        text_feat.reshape(-1, text_feat.shape[2]), text_proj, preferred_element_type=jnp.float32
    ).reshape(2, 2, 2, -1, width)
    bits = [(section >> n) & 1 for n in range(3)]
    for n in range(3):
        keep = lax.dynamic_index_in_dim(part, bits[n], 2 - n, keepdims=False)
        send = lax.dynamic_index_in_dim(part, 1 - bits[n], 2 - n, keepdims=False)
        part = keep + toggled(send, "section", 1 << n, SECTIONS)
    rows = unit_rows(part).astype(jnp.bfloat16)
    for n in (2, 1, 0):
        rows = jnp.stack([rows, toggled(rows, "section", 1 << n, SECTIONS)], axis=2 - n)
    for n in range(3):
        rows = jnp.where(bits[n] == 1, jnp.flip(rows, 2 - n), rows)
    return rows.reshape(SECTIONS, -1, width)


def body(acts, attn_proj, modulation, q_gain, text_feat, text_proj, text_len, kv_index, kv_count):
    acts, weights, modulation = acts[0], attn_proj[0], modulation[0]
    sequences, tokens, width = acts.shape
    yh, z, core = (lax.axis_index(name) for name in SEQ)
    member = 2 * yh + core
    place = jnp.stack([yh, z, core]).astype(jnp.int32)

    inputs = acts.astype(jnp.float32)
    mean = jnp.mean(inputs, axis=-1, keepdims=True)
    variance = jnp.mean((inputs - mean) ** 2, axis=-1, keepdims=True)
    shift = modulation[:, 0][:, None, :].astype(jnp.float32)
    scale = modulation[:, 1][:, None, :].astype(jnp.float32)
    modulated = ((inputs - mean) * lax.rsqrt(variance + 1e-06) * (1.0 + scale) + shift).astype(
        jnp.bfloat16
    )
    own = lax.all_to_all(modulated, "z", split_axis=0, concat_axis=0, tiled=True)
    own = own.reshape(-1, width)

    onward = [(i, (i + 1) % SECTIONS) for i in range(SECTIONS)]
    packed = jnp.concatenate([modulation[:, 2], weights[3]])
    packed = lax.ppermute(packed, "section", onward)
    gate = packed[:sequences].astype(jnp.float32)[:, None, :]
    outer = packed[sequences:]

    mine = []
    for other in range(MEMBERS):
        start = jnp.bitwise_xor(member, other) * COLS
        columns = [lax.dynamic_slice_in_dim(weights[kind], start, COLS, 1) for kind in range(3)]
        columns = jnp.concatenate(columns, axis=1)
        mine.append(toggled(columns, ("yh", "core"), other, MEMBERS) if other else columns)
    mine = jnp.stack(mine)

    text_home = text_rows(text_feat, text_proj)

    near = swap(own, "core")
    across = swap(own, "yh")
    far = swap(across, "core")
    right = left = after(mine, own, packed)
    blocks = [right]
    for _ in range(3):
        right, left = moved(right, 1), moved(left, -1)
        blocks += [right, left]
    right, left = moved(right[:2], 1), moved(left[2:], -1)
    blocks += [right, left]
    outer = lax.all_gather(after(outer, blocks[3], blocks[4]), SEQ, axis=0, tiled=True)
    text = lax.all_to_all(text_home, "z", split_axis=0, concat_axis=0, tiled=True)
    text = text.reshape(-1, width)
    text_across = swap(text, "yh")
    texts = (text, swap(text, "core"), text_across, swap(text_across, "core"))

    earlier = lax.ppermute(after(acts, right, left), "section", onward)
    gain = lax.dynamic_slice_in_dim(q_gain, member * COLS, COLS, 1)
    parts = (own, near, across, far)
    made = layer(place, kv_index, kv_count, text_len, parts, blocks, texts, gain)
    made = (*made[:-1], after(made[-1], earlier))

    own_heads, other_heads = [], []
    for distance, block in zip(ORDER, made):
        route = [
            (s * RING + i, (s + 1) % SECTIONS * RING + (i + distance) % RING)
            for s in range(SECTIONS)
            for i in range(RING)
        ]
        own_heads.append(lax.ppermute(block, ("section", "z"), route))
    for half in range(2):
        for other in range(1, MEMBERS):
            block = jnp.stack([one[other] for one in own_heads[half * 4 : half * 4 + 4]])
            other_heads.append(toggled(block, ("yh", "core"), other, MEMBERS))
    fresh = finish(place, own_heads, other_heads, outer, earlier, gate)
    return fresh[None]


def solution(mesh):
    fine = Mesh(mesh.devices.reshape(SECTIONS, 2, RING, 2), ("section",) + SEQ)
    in_specs = (
        P("section", None, SEQ, None),
        P("section", None, SEQ, None),
        P("section", None, None, None),
        P("section", None),
        P(None, SEQ, "section"),
        P("section", None),
        P(),
        P(),
        P(),
    )
    out_specs = P("section", None, SEQ, None)
    return jax.shard_map(body, mesh=fine, in_specs=in_specs, out_specs=out_specs, check_vma=False)
```

```python
import math

import jax
import jax.numpy as jnp
from jax import lax
from jax.experimental import pallas as pl
from jax.experimental.pallas import tpu as pltpu
from jax.sharding import Mesh
from jax.sharding import PartitionSpec as P

HEADS = 12
HEAD_DIM = 128
MEMBERS = 4
PER = HEADS // MEMBERS
COLS = PER * HEAD_DIM
SECTIONS = 8
RING = 8
SEQ = ("yh", "z", "core")
NEG = -1e30
VMEM = pl.BlockSpec(memory_space=pltpu.VMEM)
SMEM = pl.BlockSpec(memory_space=pltpu.SMEM)
ORDER = (4, 5, 0, 1, 3, 6, 2, 7)
RING_ORDER = (0, -1, 1, -2, 2, -3, 3, 4)


def unit_rows(values):
    return values * lax.rsqrt(jnp.mean(values * values, axis=-1, keepdims=True) + 1e-06)


def flip(bit, other):
    return bit + other - 2 * bit * other


def layer_kernel(place, kv_index, kv_count, text_len, *refs):
    parts, blocks, texts, gain, refs = refs[:4], refs[4:13], refs[13:17], refs[17], refs[18:]
    outs, refs = refs[:8], refs[8:]
    xs, ws, ts, q, k, v, kc, vc, res, w_sem, t_sem, x_sem, out_sem = refs
    yh, z, core = place[0], place[1], place[2]
    rows = blocks[0].shape[1]
    tile, txt = q.shape[1], ts.shape[0]

    def lay(block, members, offset):
        source = lax.rem(z + offset + RING, RING)
        for at, member in enumerate(members):
            source_yh = flip(yh, member // 2)
            source_core = flip(core, member % 2)
            start = pl.multiple_of((source_yh * 16 + source * 2 + source_core) * rows, 16)
            pltpu.make_async_copy(block.at[at], ws.at[pl.ds(start, rows)], w_sem).start()

    for block, offset in zip(blocks[:7], RING_ORDER):
        lay(block, range(4), offset)
    lay(blocks[7], (0, 1), 4)
    lay(blocks[8], (2, 3), 4)
    loads = [pltpu.make_async_copy(one, xs.at[at], x_sem.at[at]) for at, one in enumerate(parts)]
    for load in loads:
        load.start()
    quarter = txt // 4
    text_loads = [
        pltpu.make_async_copy(one, ts.at[at * quarter : (at + 1) * quarter], t_sem.at[at])
        for at, one in enumerate(texts)
    ]
    for load in text_loads:
        load.start()
    pltpu.make_async_copy(ws, ws, w_sem).wait()

    for part, load in enumerate(loads):
        load.wait()
        made = jnp.dot(xs[part], ws[...], preferred_element_type=jnp.float32)
        slots = slice(part // 2 * 8, part // 2 * 8 + 8)
        half = slice(part % 2 * (tile // 2), (part % 2 + 1) * (tile // 2))
        for kind, out in enumerate((q, k, v)):
            for head in range(PER):
                lanes = slice(head * HEAD_DIM, (head + 1) * HEAD_DIM)
                first = kind * COLS + head * HEAD_DIM
                mine = made[:, first : first + HEAD_DIM]
                if kind < 2:
                    mine = unit_rows(mine)
                if kind == 0:
                    mine = mine * gain[:, lanes]
                out[slots, half, lanes] = mine.astype(jnp.bfloat16).reshape(
                    8, tile // 2, HEAD_DIM
                )

    for load in text_loads:
        load.wait()
    pair = jnp.dot(ts[...], ws[:, COLS:], preferred_element_type=jnp.float32)
    for head in range(PER):
        lanes = slice(head * HEAD_DIM, (head + 1) * HEAD_DIM)
        kc[:txt, lanes] = unit_rows(pair[:, lanes]).astype(jnp.bfloat16)
    vc[:txt, :] = pair[:, COLS:].astype(jnp.bfloat16)

    scale = math.log2(math.e) / math.sqrt(HEAD_DIM)
    row = lax.broadcasted_iota(jnp.int32, (1, txt), 1)
    row_yh = flip(row // 128, yh)
    row_core = flip((row // 64) % 2, core)
    token = (row_yh * 16 + ((row // 8) % 8) * 2 + row_core) * 8 + row % 8
    bias = jnp.where(token < text_len[z], 0.0, NEG)
    contract = (((1,), (1,)), ((), ()))
    sends = [
        pltpu.make_async_copy(res.at[at], out, out_sem.at[at]) for at, out in enumerate(outs)
    ]

    def one_tile(step, carry):
        at, ry = step // 2, step % 2
        home = lax.rem(z + place[3 + at], RING)
        slot = ry * 8 + home
        index = flip(yh, ry) * 8 + home
        count = kv_count[index]
        for c in range(4):

            @pl.when(c < count)
            def _(c=c):
                near = lax.rem(kv_index[index, c] + 8 * yh, 16)
                here = slice(txt + c * tile, txt + (c + 1) * tile)
                kc[here, :] = k[near]
                vc[here, :] = v[near]

        for n in range(1, 5):

            @pl.when(count == n)
            def _(n=n):
                size = txt + n * tile
                heads = [slice(head * HEAD_DIM, (head + 1) * HEAD_DIM) for head in range(PER)]
                scores = [
                    lax.dot_general(
                        q[slot, :, lanes],
                        kc[:size, lanes],
                        contract,
                        preferred_element_type=jnp.float32,
                    )
                    for lanes in heads
                ]
                scores = [
                    jnp.concatenate([one[:, :txt] * scale + bias, one[:, txt:] * scale], axis=1)
                    for one in scores
                ]
                tops = [jnp.max(one, axis=-1, keepdims=True) for one in scores]
                exps = [jnp.exp2(one - top) for one, top in zip(scores, tops)]
                inverses = [1.0 / jnp.sum(one, axis=-1, keepdims=True) for one in exps]
                probs = [
                    (one * inverse).astype(jnp.bfloat16) for one, inverse in zip(exps, inverses)
                ]
                mixed = [
                    jnp.dot(one, vc[:size, lanes], preferred_element_type=jnp.float32)
                    for one, lanes in zip(probs, heads)
                ]
                for one, lanes in zip(mixed, heads):
                    one = one.astype(jnp.bfloat16)
                    res[at, 2 * ry, :, lanes] = one[: tile // 2]
                    res[at, 2 * ry + 1, :, lanes] = one[tile // 2 :]

        for which, send in enumerate(sends):

            @pl.when(step == 2 * which + 1)
            def _(send=send):
                send.start()

        return carry

    lax.fori_loop(0, 16, one_tile, 0)
    for send in sends:
        send.wait()


def layer(place, kv_index, kv_count, text_len, parts, blocks, texts, gain):
    rows, width = parts[0].shape
    txt = 4 * texts[0].shape[0]
    tile = 128
    hbm = pl.BlockSpec(memory_space=pl.ANY)
    order = jnp.array(ORDER, jnp.int32)
    out = jax.ShapeDtypeStruct((MEMBERS, tile // 2, COLS), jnp.bfloat16)
    heads = pltpu.VMEM((16, tile, COLS), jnp.bfloat16)
    near = pltpu.VMEM((txt + 4 * tile, COLS), jnp.bfloat16)
    return pl.pallas_call(
        layer_kernel,
        out_shape=(out,) * 8,
        in_specs=[SMEM] * 4 + [hbm] * 17 + [VMEM],
        out_specs=(hbm,) * 8,
        scratch_shapes=[
            pltpu.VMEM((4, rows, width), jnp.bfloat16),
            pltpu.VMEM((width, 3 * COLS), jnp.bfloat16),
            pltpu.VMEM((txt, width), jnp.bfloat16),
            heads,
            heads,
            heads,
            near,
            near,
            pltpu.VMEM((8, MEMBERS, tile // 2, COLS), jnp.bfloat16),
            pltpu.SemaphoreType.DMA,
            pltpu.SemaphoreType.DMA((4,)),
            pltpu.SemaphoreType.DMA((4,)),
            pltpu.SemaphoreType.DMA((8,)),
        ],
        compiler_params=pltpu.CompilerParams(vmem_limit_bytes=48 * 2**20),
        cost_estimate=pl.CostEstimate(
            flops=12 * 10**9, bytes_accessed=14 * 2**20, transcendentals=5 * 10**6
        ),
        name="layer",
    )(jnp.concatenate([place, order]), kv_index, kv_count, text_len, *parts, *blocks, *texts, gain)


def finish_kernel(place, *refs):
    own, others = refs[:8], refs[8:14]
    wo_from, acts_from, gate, out, xs, wo, acts, x_sem, wo_sem, acts_sem = refs[14:]
    yh, z, core = place[0], place[1], place[2]
    pltpu.make_async_copy(wo_from, wo, wo_sem).start()
    for other in range(MEMBERS):
        heads = flip(yh, other // 2) * 2 + flip(core, other % 2)
        lanes = pl.ds(pl.multiple_of(heads * COLS, 128), COLS)
        for at in range(8):
            if other == 0:
                block = own[at].at[0]
            else:
                block = others[(at // 4) * 3 + other - 1].at[at % 4]
            pltpu.make_async_copy(block, xs.at[pl.ds(at * 64, 64), lanes], x_sem).start()
    pltpu.make_async_copy(acts_from, acts, acts_sem).start()
    pltpu.make_async_copy(xs, xs, x_sem).wait()
    pltpu.make_async_copy(wo_from, wo, wo_sem).wait()
    pltpu.make_async_copy(acts_from, acts, acts_sem).wait()
    width = wo.shape[1]
    chunk = width // 3
    for piece in range(3):
        lanes = slice(piece * chunk, (piece + 1) * chunk)
        made = jnp.dot(xs[...], wo[:, lanes], preferred_element_type=jnp.float32)
        for at, distance in enumerate(ORDER):
            sequence = lax.rem(z - distance + RING, RING)
            out[sequence, :, lanes] = (
                acts[sequence, :, lanes].astype(jnp.float32)
                + gate[sequence, :, lanes] * made[at * 64 : (at + 1) * 64]
            ).astype(jnp.bfloat16)


def finish(place, own, others, wo, acts, gate):
    hbm = pl.BlockSpec(memory_space=pl.ANY)
    return pl.pallas_call(
        finish_kernel,
        out_shape=jax.ShapeDtypeStruct(acts.shape, jnp.bfloat16),
        in_specs=[SMEM] + [hbm] * 16 + [VMEM],
        out_specs=VMEM,
        scratch_shapes=[
            pltpu.VMEM((512, wo.shape[0]), jnp.bfloat16),
            pltpu.VMEM(wo.shape, jnp.bfloat16),
            pltpu.VMEM(acts.shape, jnp.bfloat16),
            pltpu.SemaphoreType.DMA,
            pltpu.SemaphoreType.DMA,
            pltpu.SemaphoreType.DMA,
        ],
        compiler_params=pltpu.CompilerParams(vmem_limit_bytes=40 * 2**20),
        cost_estimate=pl.CostEstimate(
            flops=2 * 512 * 1536 * 1536, bytes_accessed=12 * 2**20, transcendentals=0
        ),
        name="finish",
    )(place, *own, *others, wo, acts, gate)


def swap(block, axis):
    return lax.ppermute(block, axis, [(0, 1), (1, 0)])


def toggled(block, axis, bits, size):
    return lax.ppermute(block, axis, [(i, i ^ bits) for i in range(size)])


def moved(block, distance):
    return lax.ppermute(block, "z", [(i, (i + distance) % RING) for i in range(RING)])


def after(block, *earlier):
    for one in earlier:
        block = block + (one[(0,) * one.ndim] * 0).astype(block.dtype)
    return block


def text_rows(text_feat, text_proj):
    section = lax.axis_index("section")
    width = text_proj.shape[1]
    part = jnp.dot(
        text_feat.reshape(-1, text_feat.shape[2]), text_proj, preferred_element_type=jnp.float32
    ).reshape(2, 2, 2, -1, width)
    bits = [(section >> n) & 1 for n in range(3)]
    for n in range(3):
        keep = lax.dynamic_index_in_dim(part, bits[n], 2 - n, keepdims=False)
        send = lax.dynamic_index_in_dim(part, 1 - bits[n], 2 - n, keepdims=False)
        part = keep + toggled(send, "section", 1 << n, SECTIONS)
    rows = unit_rows(part).astype(jnp.bfloat16)
    for n in (2, 1, 0):
        rows = jnp.stack([rows, toggled(rows, "section", 1 << n, SECTIONS)], axis=2 - n)
    for n in range(3):
        rows = jnp.where(bits[n] == 1, jnp.flip(rows, 2 - n), rows)
    return rows.reshape(SECTIONS, -1, width)


def body(acts, attn_proj, modulation, q_gain, text_feat, text_proj, text_len, kv_index, kv_count):
    acts, weights, modulation = acts[0], attn_proj[0], modulation[0]
    sequences, tokens, width = acts.shape
    yh, z, core = (lax.axis_index(name) for name in SEQ)
    member = 2 * yh + core
    place = jnp.stack([yh, z, core]).astype(jnp.int32)

    inputs = acts.astype(jnp.float32)
    mean = jnp.mean(inputs, axis=-1, keepdims=True)
    variance = jnp.mean((inputs - mean) ** 2, axis=-1, keepdims=True)
    shift = modulation[:, 0][:, None, :].astype(jnp.float32)
    scale = modulation[:, 1][:, None, :].astype(jnp.float32)
    modulated = ((inputs - mean) * lax.rsqrt(variance + 1e-06) * (1.0 + scale) + shift).astype(
        jnp.bfloat16
    )
    own = lax.all_to_all(modulated, "z", split_axis=0, concat_axis=0, tiled=True)
    own = own.reshape(-1, width)

    onward = [(i, (i + 1) % SECTIONS) for i in range(SECTIONS)]
    packed = jnp.concatenate([modulation[:, 2], weights[3]])
    packed = lax.ppermute(packed, "section", onward)
    gate = packed[:sequences].astype(jnp.float32)[:, None, :]
    outer = packed[sequences:]

    mine = []
    for other in range(MEMBERS):
        start = jnp.bitwise_xor(member, other) * COLS
        columns = [lax.dynamic_slice_in_dim(weights[kind], start, COLS, 1) for kind in range(3)]
        columns = jnp.concatenate(columns, axis=1)
        mine.append(toggled(columns, ("yh", "core"), other, MEMBERS) if other else columns)
    mine = jnp.stack(mine)

    text_home = text_rows(text_feat, text_proj)

    own = after(own, text_home, mine, packed)
    across = swap(own, "yh")
    near = swap(own, "core")
    far = swap(across, "core")
    text = lax.all_to_all(text_home, "z", split_axis=0, concat_axis=0, tiled=True)
    text = text.reshape(-1, width)
    right = left = after(mine, own)
    blocks = [right]
    for step in range(3):
        if step == 2:
            right, left = after(right, text), after(left, text)
        right, left = moved(right, 1), moved(left, -1)
        blocks += [right, left]
    right, left = moved(right[:2], 1), moved(left[2:], -1)
    blocks += [right, left]
    text_across = swap(text, "yh")
    texts = (text, swap(text, "core"), text_across, swap(text_across, "core"))

    earlier = lax.ppermute(after(acts, right, left, texts[3]), "section", onward)
    outer = lax.all_gather(after(outer, right, left), SEQ, axis=0, tiled=True)
    gain = lax.dynamic_slice_in_dim(q_gain, member * COLS, COLS, 1)
    parts = (own, near, across, far)
    made = layer(place, kv_index, kv_count, text_len, parts, blocks, texts, gain)
    first = made[0][0, 0, 0]
    look = lax.dynamic_index_in_dim(earlier, (first != first).astype(jnp.int32), 0)
    made = (*made[:-1], after(made[-1], look))

    own_heads, other_heads = [], []
    for distance, block in zip(ORDER, made):
        route = [
            (s * RING + i, (s + 1) % SECTIONS * RING + (i + distance) % RING)
            for s in range(SECTIONS)
            for i in range(RING)
        ]
        own_heads.append(lax.ppermute(block, ("section", "z"), route))
    for half in range(2):
        for other in range(1, MEMBERS):
            block = jnp.stack([one[other] for one in own_heads[half * 4 : half * 4 + 4]])
            other_heads.append(toggled(block, ("yh", "core"), other, MEMBERS))
    fresh = finish(place, own_heads, other_heads, outer, earlier, gate)
    return fresh[None]


def solution(mesh):
    fine = Mesh(mesh.devices.reshape(SECTIONS, 2, RING, 2), ("section",) + SEQ)
    in_specs = (
        P("section", None, SEQ, None),
        P("section", None, SEQ, None),
        P("section", None, None, None),
        P("section", None),
        P(None, SEQ, "section"),
        P("section", None),
        P(),
        P(),
        P(),
    )
    out_specs = P("section", None, SEQ, None)
    return jax.shard_map(body, mesh=fine, in_specs=in_specs, out_specs=out_specs, check_vma=False)
```

```python
import math

import jax
import jax.numpy as jnp
from jax import lax
from jax.experimental import pallas as pl
from jax.experimental.pallas import tpu as pltpu
from jax.sharding import Mesh
from jax.sharding import PartitionSpec as P

HEADS = 12
HEAD_DIM = 128
MEMBERS = 4
PER = HEADS // MEMBERS
COLS = PER * HEAD_DIM
SECTIONS = 8
RING = 8
SEQ = ("yh", "z", "core")
NEG = -1e30
ROOM = 60 * 2**20
VMEM = pl.BlockSpec(memory_space=pltpu.VMEM)
SMEM = pl.BlockSpec(memory_space=pltpu.SMEM)
ORDER = (4, 5, 0, 1, 3, 6, 2, 7)
RING_ORDER = (0, -1, 1, -2, 2, -3, 3, 4)


def unit_rows(values):
    return values * lax.rsqrt(jnp.mean(values * values, axis=-1, keepdims=True) + 1e-06)


def flip(bit, other):
    return bit + other - 2 * bit * other


def modulate_kernel(acts, modulation, out):
    inputs = acts[0].astype(jnp.float32)
    mean = jnp.mean(inputs, axis=-1, keepdims=True)
    centred = inputs - mean
    variance = jnp.mean(centred * centred, axis=-1, keepdims=True)
    shift = modulation[0, 0:1, :].astype(jnp.float32)
    scale = modulation[0, 1:2, :].astype(jnp.float32)
    out[0] = (centred * lax.rsqrt(variance + 1e-06) * (1.0 + scale) + shift).astype(jnp.bfloat16)


def modulate(acts, modulation):
    sequences, tokens, width = acts.shape
    rows = pl.BlockSpec((1, tokens, width), lambda i: (i, 0, 0))
    return pl.pallas_call(
        modulate_kernel,
        grid=(sequences,),
        out_shape=jax.ShapeDtypeStruct(acts.shape, acts.dtype),
        in_specs=[rows, pl.BlockSpec((1, 3, width), lambda i: (i, 0, 0))],
        out_specs=rows,
        compiler_params=pltpu.CompilerParams(vmem_limit_bytes=ROOM),
        cost_estimate=pl.CostEstimate(
            flops=10 * acts.size, bytes_accessed=4 * acts.size, transcendentals=0
        ),
        name="modulate",
    )(acts, modulation)


def hold_kernel(*refs):
    del refs


def hold(arrays, earlier=(), flops=0):
    hbm = pl.BlockSpec(memory_space=pl.ANY)
    return pl.pallas_call(
        hold_kernel,
        out_shape=[jax.ShapeDtypeStruct(one.shape, one.dtype) for one in arrays],
        in_specs=[hbm] * (len(arrays) + len(earlier)),
        out_specs=[hbm] * len(arrays),
        input_output_aliases={at: at for at in range(len(arrays))},
        compiler_params=pltpu.CompilerParams(vmem_limit_bytes=ROOM),
        cost_estimate=pl.CostEstimate(flops=flops, bytes_accessed=0, transcendentals=0),
        name="hold",
    )(*arrays, *earlier)


def layer_kernel(place, kv_index, kv_count, text_len, *refs):
    parts, blocks, texts, gain, refs = refs[:4], refs[4:13], refs[13:17], refs[17], refs[18:]
    outs, refs = refs[:8], refs[8:]
    xs, ws, ts, q, k, v, kc, vc, res, w_sem, t_sem, x_sem, out_sem = refs
    yh, z, core = place[0], place[1], place[2]
    rows = blocks[0].shape[1]
    tile, txt = q.shape[1], ts.shape[0]

    def lay(block, members, offset):
        source = lax.rem(z + offset + RING, RING)
        for at, member in enumerate(members):
            source_yh = flip(yh, member // 2)
            source_core = flip(core, member % 2)
            start = pl.multiple_of((source_yh * 16 + source * 2 + source_core) * rows, 16)
            pltpu.make_async_copy(block.at[at], ws.at[pl.ds(start, rows)], w_sem).start()

    for block, offset in zip(blocks[:7], RING_ORDER):
        lay(block, range(4), offset)
    lay(blocks[7], (0, 1), 4)
    lay(blocks[8], (2, 3), 4)
    loads = [pltpu.make_async_copy(one, xs.at[at], x_sem.at[at]) for at, one in enumerate(parts)]
    for load in loads:
        load.start()
    quarter = txt // 4
    text_loads = [
        pltpu.make_async_copy(one, ts.at[at * quarter : (at + 1) * quarter], t_sem.at[at])
        for at, one in enumerate(texts)
    ]
    for load in text_loads:
        load.start()
    pltpu.make_async_copy(ws, ws, w_sem).wait()

    for part, load in enumerate(loads):
        load.wait()
        made = jnp.dot(xs[part], ws[...], preferred_element_type=jnp.float32)
        slots = slice(part // 2 * 8, part // 2 * 8 + 8)
        half = slice(part % 2 * (tile // 2), (part % 2 + 1) * (tile // 2))
        for kind, out in enumerate((q, k, v)):
            for head in range(PER):
                lanes = slice(head * HEAD_DIM, (head + 1) * HEAD_DIM)
                first = kind * COLS + head * HEAD_DIM
                mine = made[:, first : first + HEAD_DIM]
                if kind < 2:
                    mine = unit_rows(mine)
                if kind == 0:
                    mine = mine * gain[:, lanes]
                out[slots, half, lanes] = mine.astype(jnp.bfloat16).reshape(
                    8, tile // 2, HEAD_DIM
                )

    for load in text_loads:
        load.wait()
    pair = jnp.dot(ts[...], ws[:, COLS:], preferred_element_type=jnp.float32)
    for head in range(PER):
        lanes = slice(head * HEAD_DIM, (head + 1) * HEAD_DIM)
        kc[:txt, lanes] = unit_rows(pair[:, lanes]).astype(jnp.bfloat16)
    vc[:txt, :] = pair[:, COLS:].astype(jnp.bfloat16)

    scale = math.log2(math.e) / math.sqrt(HEAD_DIM)
    row = lax.broadcasted_iota(jnp.int32, (1, txt), 1)
    row_yh = flip(row // 128, yh)
    row_core = flip((row // 64) % 2, core)
    row_z = jnp.bitwise_xor((row // 8) % 8, place[11])
    token = (row_yh * 16 + row_z * 2 + row_core) * 8 + row % 8
    bias = jnp.where(token < text_len[z], 0.0, NEG)
    contract = (((1,), (1,)), ((), ()))
    sends = [
        pltpu.make_async_copy(res.at[at], out, out_sem.at[at]) for at, out in enumerate(outs)
    ]

    def one_tile(step, carry):
        at, ry = step // 2, step % 2
        home = lax.rem(z + place[3 + at], RING)
        slot = ry * 8 + home
        index = flip(yh, ry) * 8 + home
        count = kv_count[index]
        for c in range(4):

            @pl.when(c < count)
            def _(c=c):
                near = lax.rem(kv_index[index, c] + 8 * yh, 16)
                here = slice(txt + c * tile, txt + (c + 1) * tile)
                kc[here, :] = k[near]
                vc[here, :] = v[near]

        for n in range(1, 5):

            @pl.when(count == n)
            def _(n=n):
                size = txt + n * tile
                heads = [slice(head * HEAD_DIM, (head + 1) * HEAD_DIM) for head in range(PER)]
                scores = [
                    lax.dot_general(
                        q[slot, :, lanes],
                        kc[:size, lanes],
                        contract,
                        preferred_element_type=jnp.float32,
                    )
                    for lanes in heads
                ]
                scores = [
                    jnp.concatenate([one[:, :txt] * scale + bias, one[:, txt:] * scale], axis=1)
                    for one in scores
                ]
                tops = [jnp.max(one, axis=-1, keepdims=True) for one in scores]
                exps = [jnp.exp2(one - top) for one, top in zip(scores, tops)]
                inverses = [1.0 / jnp.sum(one, axis=-1, keepdims=True) for one in exps]
                probs = [
                    (one * inverse).astype(jnp.bfloat16) for one, inverse in zip(exps, inverses)
                ]
                mixed = [
                    jnp.dot(one, vc[:size, lanes], preferred_element_type=jnp.float32)
                    for one, lanes in zip(probs, heads)
                ]
                for one, lanes in zip(mixed, heads):
                    one = one.astype(jnp.bfloat16)
                    res[at, 2 * ry, :, lanes] = one[: tile // 2]
                    res[at, 2 * ry + 1, :, lanes] = one[tile // 2 :]

        for which, send in enumerate(sends):

            @pl.when(step == 2 * which + 1)
            def _(send=send):
                send.start()

        return carry

    lax.fori_loop(0, 16, one_tile, 0)
    for send in sends:
        send.wait()


def layer(place, section, kv_index, kv_count, text_len, parts, blocks, texts, gain):
    rows, width = parts[0].shape
    txt = 4 * texts[0].shape[0]
    tile = 128
    hbm = pl.BlockSpec(memory_space=pl.ANY)
    order = jnp.array(ORDER, jnp.int32)
    out = jax.ShapeDtypeStruct((MEMBERS, tile // 2, COLS), jnp.bfloat16)
    heads = pltpu.VMEM((16, tile, COLS), jnp.bfloat16)
    near = pltpu.VMEM((txt + 4 * tile, COLS), jnp.bfloat16)
    return pl.pallas_call(
        layer_kernel,
        out_shape=(out,) * 8,
        in_specs=[SMEM] * 4 + [hbm] * 17 + [VMEM],
        out_specs=(hbm,) * 8,
        scratch_shapes=[
            pltpu.VMEM((4, rows, width), jnp.bfloat16),
            pltpu.VMEM((width, 3 * COLS), jnp.bfloat16),
            pltpu.VMEM((txt, width), jnp.bfloat16),
            heads,
            heads,
            heads,
            near,
            near,
            pltpu.VMEM((8, MEMBERS, tile // 2, COLS), jnp.bfloat16),
            pltpu.SemaphoreType.DMA,
            pltpu.SemaphoreType.DMA((4,)),
            pltpu.SemaphoreType.DMA((4,)),
            pltpu.SemaphoreType.DMA((8,)),
        ],
        compiler_params=pltpu.CompilerParams(vmem_limit_bytes=ROOM),
        cost_estimate=pl.CostEstimate(
            flops=5 * 10**10, bytes_accessed=14 * 2**20, transcendentals=5 * 10**6
        ),
        name="layer",
    )(jnp.concatenate([place, order, section[None]]), kv_index, kv_count, text_len, *parts, *blocks, *texts, gain)


def finish_kernel(place, *refs):
    own, others = refs[:8], refs[8:14]
    wo_from, acts_from, gate, out, xs, wo, acts, x_sem, wo_sem, acts_sem = refs[14:]
    yh, z, core = place[0], place[1], place[2]
    pltpu.make_async_copy(wo_from, wo, wo_sem).start()
    for other in range(MEMBERS):
        heads = flip(yh, other // 2) * 2 + flip(core, other % 2)
        lanes = pl.ds(pl.multiple_of(heads * COLS, 128), COLS)
        for at in range(8):
            if other == 0:
                block = own[at].at[0]
            else:
                block = others[(at // 4) * 3 + other - 1].at[at % 4]
            pltpu.make_async_copy(block, xs.at[pl.ds(at * 64, 64), lanes], x_sem).start()
    pltpu.make_async_copy(acts_from, acts, acts_sem).start()
    pltpu.make_async_copy(xs, xs, x_sem).wait()
    pltpu.make_async_copy(wo_from, wo, wo_sem).wait()
    pltpu.make_async_copy(acts_from, acts, acts_sem).wait()
    width = wo.shape[1]
    chunk = width // 3
    for piece in range(3):
        lanes = slice(piece * chunk, (piece + 1) * chunk)
        made = jnp.dot(xs[...], wo[:, lanes], preferred_element_type=jnp.float32)
        for at, distance in enumerate(ORDER):
            sequence = lax.rem(z - distance + RING, RING)
            out[sequence, :, lanes] = (
                acts[sequence, :, lanes].astype(jnp.float32)
                + gate[sequence, :, lanes] * made[at * 64 : (at + 1) * 64]
            ).astype(jnp.bfloat16)


def finish(place, own, others, wo, acts, gate):
    hbm = pl.BlockSpec(memory_space=pl.ANY)
    return pl.pallas_call(
        finish_kernel,
        out_shape=jax.ShapeDtypeStruct(acts.shape, jnp.bfloat16),
        in_specs=[SMEM] + [hbm] * 16 + [VMEM],
        out_specs=VMEM,
        scratch_shapes=[
            pltpu.VMEM((512, wo.shape[0]), jnp.bfloat16),
            pltpu.VMEM(wo.shape, jnp.bfloat16),
            pltpu.VMEM(acts.shape, jnp.bfloat16),
            pltpu.SemaphoreType.DMA,
            pltpu.SemaphoreType.DMA,
            pltpu.SemaphoreType.DMA,
        ],
        compiler_params=pltpu.CompilerParams(vmem_limit_bytes=ROOM),
        cost_estimate=pl.CostEstimate(
            flops=2 * 512 * 1536 * 1536, bytes_accessed=12 * 2**20, transcendentals=0
        ),
        name="finish",
    )(place, *own, *others, wo, acts, gate)


def swap(block, axis):
    return lax.ppermute(block, axis, [(0, 1), (1, 0)])


def toggled(block, axis, bits, size):
    return lax.ppermute(block, axis, [(i, i ^ bits) for i in range(size)])


def moved(block, distance):
    return lax.ppermute(block, "z", [(i, (i + distance) % RING) for i in range(RING)])


def text_rows(text_feat, text_proj):
    section = lax.axis_index("section")
    width = text_proj.shape[1]
    part = jnp.dot(
        text_feat.reshape(-1, text_feat.shape[2]), text_proj, preferred_element_type=jnp.float32
    ).reshape(2, 2, 2, -1, width)
    bits = [(section >> n) & 1 for n in range(3)]
    for n in range(3):
        keep = lax.dynamic_index_in_dim(part, bits[n], 2 - n, keepdims=False)
        send = lax.dynamic_index_in_dim(part, 1 - bits[n], 2 - n, keepdims=False)
        part = keep + toggled(send, "section", 1 << n, SECTIONS)
    rows = unit_rows(part).astype(jnp.bfloat16)
    for n in (2, 1, 0):
        rows = jnp.stack([rows, toggled(rows, "z", 1 << n, RING)], axis=2 - n)
    route = [(s * RING + i, i * RING + s) for s in range(SECTIONS) for i in range(RING)]
    return lax.ppermute(rows.reshape(-1, width), ("section", "z"), route)


def body(acts, attn_proj, modulation, q_gain, text_feat, text_proj, text_len, kv_index, kv_count):
    acts, weights, modulation = acts[0], attn_proj[0], modulation[0]
    sequences, tokens, width = acts.shape
    yh, z, core = (lax.axis_index(name) for name in SEQ)
    member = 2 * yh + core
    place = jnp.stack([yh, z, core]).astype(jnp.int32)

    modulated = modulate(acts, modulation)
    own = lax.all_to_all(modulated, "z", split_axis=0, concat_axis=0, tiled=True)
    own = own.reshape(-1, width)

    onward = [(i, (i + 1) % SECTIONS) for i in range(SECTIONS)]
    packed = jnp.concatenate([modulation[:, 2], weights[3]])
    packed = lax.ppermute(packed, "section", onward)
    gate = packed[:sequences].astype(jnp.float32)[:, None, :]
    outer = packed[sequences:]

    mine = []
    for other in range(MEMBERS):
        start = jnp.bitwise_xor(member, other) * COLS
        columns = [lax.dynamic_slice_in_dim(weights[kind], start, COLS, 1) for kind in range(3)]
        columns = jnp.concatenate(columns, axis=1)
        mine.append(toggled(columns, ("yh", "core"), other, MEMBERS) if other else columns)
    mine = jnp.stack(mine)

    text = text_rows(text_feat, text_proj)

    (own,) = hold([own], [text, mine, packed])
    across = swap(own, "yh")
    near = swap(own, "core")
    text_across = swap(text, "yh")
    texts = (text, swap(text, "core"), text_across, swap(text_across, "core"))
    (mine,) = hold([mine], [own], 10**11)
    right = left = mine
    blocks = [mine]
    for step in range(3):
        right, left = moved(right, 1), moved(left, -1)
        if step == 1:
            right, left = hold([right, left], [text_across])
        blocks += [right, left]
    right, left = moved(right[:2], 1), moved(left[2:], -1)
    blocks += [right, left]

    across, outer = hold([across, outer], [right, left])
    far = swap(across, "core")
    earlier = lax.ppermute(acts, "section", onward)
    outer = lax.all_gather(outer, SEQ, axis=0, tiled=True)
    gain = lax.dynamic_slice_in_dim(q_gain, member * COLS, COLS, 1)
    parts = (own, near, across, far)
    section = lax.axis_index("section").astype(jnp.int32)
    made = layer(place, section, kv_index, kv_count, text_len, parts, blocks, texts, gain)
    made = (*made[:-1], *hold([made[-1]], [earlier]))

    own_heads, other_heads = [], []
    for distance, block in zip(ORDER, made):
        route = [
            (s * RING + i, (s + 1) % SECTIONS * RING + (i + distance) % RING)
            for s in range(SECTIONS)
            for i in range(RING)
        ]
        own_heads.append(lax.ppermute(block, ("section", "z"), route))
    for half in range(2):
        for other in range(1, MEMBERS):
            block = jnp.stack([one[other] for one in own_heads[half * 4 : half * 4 + 4]])
            other_heads.append(toggled(block, ("yh", "core"), other, MEMBERS))
    fresh = finish(place, own_heads, other_heads, outer, earlier, gate)
    return fresh[None]


def solution(mesh):
    fine = Mesh(mesh.devices.reshape(SECTIONS, 2, RING, 2), ("section",) + SEQ)
    in_specs = (
        P("section", None, SEQ, None),
        P("section", None, SEQ, None),
        P("section", None, None, None),
        P("section", None),
        P(None, SEQ, "section"),
        P("section", None),
        P(),
        P(),
        P(),
    )
    out_specs = P("section", None, SEQ, None)
    return jax.shard_map(body, mesh=fine, in_specs=in_specs, out_specs=out_specs, check_vma=False)
```

```python
import math

import jax
import jax.numpy as jnp
from jax import lax
from jax.experimental import pallas as pl
from jax.experimental.pallas import tpu as pltpu
from jax.sharding import Mesh
from jax.sharding import PartitionSpec as P

HEADS = 12
HEAD_DIM = 128
MEMBERS = 4
PER = HEADS // MEMBERS
COLS = PER * HEAD_DIM
SECTIONS = 8
RING = 8
SEQ = ("yh", "z", "core")
NEG = -1e30
ROOM = 60 * 2**20
VMEM = pl.BlockSpec(memory_space=pltpu.VMEM)
SMEM = pl.BlockSpec(memory_space=pltpu.SMEM)
ORDER = (4, 5, 0, 1, 3, 6, 2, 7)
RING_ORDER = (0, -1, 1, -2, 2, -3, 3, 4)


def unit_rows(values):
    return values * lax.rsqrt(jnp.mean(values * values, axis=-1, keepdims=True) + 1e-06)


def flip(bit, other):
    return bit + other - 2 * bit * other


def modulate_kernel(acts, modulation, out):
    inputs = acts[0].astype(jnp.float32)
    mean = jnp.mean(inputs, axis=-1, keepdims=True)
    centred = inputs - mean
    variance = jnp.mean(centred * centred, axis=-1, keepdims=True)
    shift = modulation[0, 0:1, :].astype(jnp.float32)
    scale = modulation[0, 1:2, :].astype(jnp.float32)
    out[0] = (centred * lax.rsqrt(variance + 1e-06) * (1.0 + scale) + shift).astype(jnp.bfloat16)


def modulate(acts, modulation):
    sequences, tokens, width = acts.shape
    rows = pl.BlockSpec((1, tokens, width), lambda i: (i, 0, 0))
    return pl.pallas_call(
        modulate_kernel,
        grid=(sequences,),
        out_shape=jax.ShapeDtypeStruct(acts.shape, acts.dtype),
        in_specs=[rows, pl.BlockSpec((1, 3, width), lambda i: (i, 0, 0))],
        out_specs=rows,
        compiler_params=pltpu.CompilerParams(vmem_limit_bytes=ROOM),
        cost_estimate=pl.CostEstimate(
            flops=10**11, bytes_accessed=4 * acts.size, transcendentals=0
        ),
        name="modulate",
    )(acts, modulation)


def hold_kernel(*refs):
    del refs


def hold(arrays, earlier=(), flops=0):
    hbm = pl.BlockSpec(memory_space=pl.ANY)
    return pl.pallas_call(
        hold_kernel,
        out_shape=[jax.ShapeDtypeStruct(one.shape, one.dtype) for one in arrays],
        in_specs=[hbm] * (len(arrays) + len(earlier)),
        out_specs=[hbm] * len(arrays),
        input_output_aliases={at: at for at in range(len(arrays))},
        compiler_params=pltpu.CompilerParams(vmem_limit_bytes=ROOM),
        cost_estimate=pl.CostEstimate(flops=flops, bytes_accessed=0, transcendentals=0),
        name="hold",
    )(*arrays, *earlier)


def layer_kernel(place, kv_index, kv_count, text_len, *refs):
    parts, blocks, gain, refs = refs[:4], refs[4:13], refs[13], refs[14:]
    outs, refs = refs[:8], refs[8:]
    xs, ws, ts, q, k, v, kc, vc, res, w_sem, t_sem, x_sem, out_sem = refs
    yh, z, core = place[0], place[1], place[2]
    rows = blocks[0].shape[1]
    tile, txt = q.shape[1], ts.shape[0]

    def lay(block, members, offset):
        source = lax.rem(z + offset + RING, RING)
        for at, member in enumerate(members):
            source_yh = flip(yh, member // 2)
            source_core = flip(core, member % 2)
            start = pl.multiple_of((source_yh * 16 + source * 2 + source_core) * rows, 16)
            pltpu.make_async_copy(
                block.at[at, :, : 3 * COLS], ws.at[pl.ds(start, rows)], w_sem
            ).start()

    for block, offset in zip(blocks[:7], RING_ORDER):
        lay(block, range(4), offset)
    lay(blocks[7], (0, 1), 4)
    lay(blocks[8], (2, 3), 4)
    own, quarter = xs.shape[1], txt // 4
    loads = [
        pltpu.make_async_copy(one.at[:own], xs.at[at], x_sem.at[at])
        for at, one in enumerate(parts)
    ]
    text_loads = [
        pltpu.make_async_copy(
            one.at[own:], ts.at[at * quarter : (at + 1) * quarter], t_sem.at[at]
        )
        for at, one in enumerate(parts)
    ]
    for load in loads + text_loads:
        load.start()
    pltpu.make_async_copy(ws, ws, w_sem).wait()

    for part, load in enumerate(loads):
        load.wait()
        made = jnp.dot(xs[part], ws[...], preferred_element_type=jnp.float32)
        slots = slice(part // 2 * 8, part // 2 * 8 + 8)
        half = slice(part % 2 * (tile // 2), (part % 2 + 1) * (tile // 2))
        for kind, out in enumerate((q, k, v)):
            for head in range(PER):
                lanes = slice(head * HEAD_DIM, (head + 1) * HEAD_DIM)
                first = kind * COLS + head * HEAD_DIM
                mine = made[:, first : first + HEAD_DIM]
                if kind < 2:
                    mine = unit_rows(mine)
                if kind == 0:
                    mine = mine * gain[:, lanes]
                out[slots, half, lanes] = mine.astype(jnp.bfloat16).reshape(
                    8, tile // 2, HEAD_DIM
                )

    for load in text_loads:
        load.wait()
    pair = jnp.dot(ts[...], ws[:, COLS:], preferred_element_type=jnp.float32)
    for head in range(PER):
        lanes = slice(head * HEAD_DIM, (head + 1) * HEAD_DIM)
        kc[:txt, lanes] = unit_rows(pair[:, lanes]).astype(jnp.bfloat16)
    vc[:txt, :] = pair[:, COLS:].astype(jnp.bfloat16)

    scale = math.log2(math.e) / math.sqrt(HEAD_DIM)
    row = lax.broadcasted_iota(jnp.int32, (1, txt), 1)
    row_yh = flip(row // 128, yh)
    row_core = flip((row // 64) % 2, core)
    token = (row_yh * 16 + ((row // 8) % 8) * 2 + row_core) * 8 + row % 8
    bias = jnp.where(token < text_len[z], 0.0, NEG)
    contract = (((1,), (1,)), ((), ()))
    sends = [
        pltpu.make_async_copy(res.at[at], out, out_sem.at[at]) for at, out in enumerate(outs)
    ]

    def one_tile(step, carry):
        at, ry = step // 2, step % 2
        home = lax.rem(z + place[3 + at], RING)
        slot = ry * 8 + home
        index = flip(yh, ry) * 8 + home
        count = kv_count[index]
        for c in range(4):

            @pl.when(c < count)
            def _(c=c):
                near = lax.rem(kv_index[index, c] + 8 * yh, 16)
                here = slice(txt + c * tile, txt + (c + 1) * tile)
                kc[here, :] = k[near]
                vc[here, :] = v[near]

        for n in range(1, 5):

            @pl.when(count == n)
            def _(n=n):
                size = txt + n * tile
                heads = [slice(head * HEAD_DIM, (head + 1) * HEAD_DIM) for head in range(PER)]
                scores = [
                    lax.dot_general(
                        q[slot, :, lanes],
                        kc[:size, lanes],
                        contract,
                        preferred_element_type=jnp.float32,
                    )
                    for lanes in heads
                ]
                scores = [
                    jnp.concatenate([one[:, :txt] * scale + bias, one[:, txt:] * scale], axis=1)
                    for one in scores
                ]
                tops = [jnp.max(one, axis=-1, keepdims=True) for one in scores]
                exps = [jnp.exp2(one - top) for one, top in zip(scores, tops)]
                inverses = [1.0 / jnp.sum(one, axis=-1, keepdims=True) for one in exps]
                probs = [
                    (one * inverse).astype(jnp.bfloat16) for one, inverse in zip(exps, inverses)
                ]
                mixed = [
                    jnp.dot(one, vc[:size, lanes], preferred_element_type=jnp.float32)
                    for one, lanes in zip(probs, heads)
                ]
                for one, lanes in zip(mixed, heads):
                    one = one.astype(jnp.bfloat16)
                    res[at, 2 * ry, :, lanes] = one[: tile // 2]
                    res[at, 2 * ry + 1, :, lanes] = one[tile // 2 :]

        for which, send in enumerate(sends):

            @pl.when(step == 2 * which + 1)
            def _(send=send):
                send.start()

        return carry

    lax.fori_loop(0, 16, one_tile, 0)
    for send in sends:
        send.wait()


def layer(place, kv_index, kv_count, text_len, parts, blocks, gain):
    width = parts[0].shape[1]
    rows = 512
    txt = 4 * (parts[0].shape[0] - rows)
    tile = 128
    hbm = pl.BlockSpec(memory_space=pl.ANY)
    order = jnp.array(ORDER, jnp.int32)
    out = jax.ShapeDtypeStruct((MEMBERS, tile // 2, COLS), jnp.bfloat16)
    heads = pltpu.VMEM((16, tile, COLS), jnp.bfloat16)
    near = pltpu.VMEM((txt + 4 * tile, COLS), jnp.bfloat16)
    return pl.pallas_call(
        layer_kernel,
        out_shape=(out,) * 8,
        in_specs=[SMEM] * 4 + [hbm] * 13 + [VMEM],
        out_specs=(hbm,) * 8,
        scratch_shapes=[
            pltpu.VMEM((4, rows, width), jnp.bfloat16),
            pltpu.VMEM((width, 3 * COLS), jnp.bfloat16),
            pltpu.VMEM((txt, width), jnp.bfloat16),
            heads,
            heads,
            heads,
            near,
            near,
            pltpu.VMEM((8, MEMBERS, tile // 2, COLS), jnp.bfloat16),
            pltpu.SemaphoreType.DMA,
            pltpu.SemaphoreType.DMA((4,)),
            pltpu.SemaphoreType.DMA((4,)),
            pltpu.SemaphoreType.DMA((8,)),
        ],
        compiler_params=pltpu.CompilerParams(vmem_limit_bytes=ROOM),
        cost_estimate=pl.CostEstimate(
            flops=5 * 10**10, bytes_accessed=14 * 2**20, transcendentals=5 * 10**6
        ),
        name="layer",
    )(jnp.concatenate([place, order]), kv_index, kv_count, text_len, *parts, *blocks, gain)


def pack_kernel(*refs):
    blocks, out, sem = refs[:9], refs[9], refs[10]
    for slot, block in enumerate(blocks[:7]):
        for group in range(4):
            lanes = slice(group * COLS, (group + 1) * COLS)
            pltpu.make_async_copy(
                block.at[group, :, 3 * COLS :], out.at[slot, :, lanes], sem
            ).start()
    for group in range(4):
        lanes = slice(group * COLS, (group + 1) * COLS)
        pltpu.make_async_copy(
            blocks[7 + group // 2].at[group % 2, :, 3 * COLS :], out.at[7, :, lanes], sem
        ).start()
    pltpu.make_async_copy(out, out, sem).wait()


def pack(blocks):
    hbm = pl.BlockSpec(memory_space=pl.ANY)
    _, rows, width = blocks[0].shape
    return pl.pallas_call(
        pack_kernel,
        out_shape=jax.ShapeDtypeStruct((RING, rows, width), jnp.bfloat16),
        in_specs=[hbm] * 9,
        out_specs=hbm,
        scratch_shapes=[pltpu.SemaphoreType.DMA],
        compiler_params=pltpu.CompilerParams(vmem_limit_bytes=ROOM),
        cost_estimate=pl.CostEstimate(flops=0, bytes_accessed=2 * 2**20, transcendentals=0),
        name="pack",
    )(*blocks)


def finish_kernel(place, *refs):
    own, others = refs[:8], refs[8:14]
    pieces, refs = refs[14:18], refs[18:]
    acts_from, gate, out, xs, wo, acts, x_sem, wo_sem, acts_sem = refs
    yh, z, core = place[0], place[1], place[2]
    rows = pieces[0].shape[1]
    for other, block in enumerate(pieces):
        for slot, offset in enumerate(RING_ORDER):
            source = lax.rem(z + offset + RING, RING)
            source_yh = flip(yh, other // 2)
            source_core = flip(core, other % 2)
            start = pl.multiple_of((source_yh * 16 + source * 2 + source_core) * rows, 16)
            pltpu.make_async_copy(block.at[slot], wo.at[pl.ds(start, rows)], wo_sem).start()
    for other in range(MEMBERS):
        heads = flip(yh, other // 2) * 2 + flip(core, other % 2)
        lanes = pl.ds(pl.multiple_of(heads * COLS, 128), COLS)
        for at in range(8):
            if other == 0:
                block = own[at].at[0]
            else:
                block = others[(at // 4) * 3 + other - 1].at[at % 4]
            pltpu.make_async_copy(block, xs.at[pl.ds(at * 64, 64), lanes], x_sem).start()
    pltpu.make_async_copy(acts_from, acts, acts_sem).start()
    pltpu.make_async_copy(xs, xs, x_sem).wait()
    pltpu.make_async_copy(wo, wo, wo_sem).wait()
    pltpu.make_async_copy(acts_from, acts, acts_sem).wait()
    width = wo.shape[1]
    chunk = width // 3
    for piece in range(3):
        lanes = slice(piece * chunk, (piece + 1) * chunk)
        made = jnp.dot(xs[...], wo[:, lanes], preferred_element_type=jnp.float32)
        for at, distance in enumerate(ORDER):
            sequence = lax.rem(z - distance + RING, RING)
            out[sequence, :, lanes] = (
                acts[sequence, :, lanes].astype(jnp.float32)
                + gate[sequence, :, lanes] * made[at * 64 : (at + 1) * 64]
            ).astype(jnp.bfloat16)


def finish(place, own, others, pieces, acts, gate):
    width = acts.shape[2]
    hbm = pl.BlockSpec(memory_space=pl.ANY)
    return pl.pallas_call(
        finish_kernel,
        out_shape=jax.ShapeDtypeStruct(acts.shape, jnp.bfloat16),
        in_specs=[SMEM] + [hbm] * 19 + [VMEM],
        out_specs=VMEM,
        scratch_shapes=[
            pltpu.VMEM((512, width), jnp.bfloat16),
            pltpu.VMEM((width, width), jnp.bfloat16),
            pltpu.VMEM(acts.shape, jnp.bfloat16),
            pltpu.SemaphoreType.DMA,
            pltpu.SemaphoreType.DMA,
            pltpu.SemaphoreType.DMA,
        ],
        compiler_params=pltpu.CompilerParams(vmem_limit_bytes=ROOM),
        cost_estimate=pl.CostEstimate(
            flops=2 * 512 * 1536 * 1536, bytes_accessed=12 * 2**20, transcendentals=0
        ),
        name="finish",
    )(place, *own, *others, *pieces, acts, gate)


def swap(block, axis):
    return lax.ppermute(block, axis, [(0, 1), (1, 0)])


def toggled(block, axis, bits, size):
    return lax.ppermute(block, axis, [(i, i ^ bits) for i in range(size)])


def moved(block, distance):
    return lax.ppermute(block, "z", [(i, (i + distance) % RING) for i in range(RING)])


def text_rows(text_feat, text_proj):
    section = lax.axis_index("section")
    width = text_proj.shape[1]
    part = jnp.dot(
        text_feat.reshape(-1, text_feat.shape[2]), text_proj, preferred_element_type=jnp.float32
    ).reshape(2, 2, 2, -1, width)
    bits = [(section >> n) & 1 for n in range(3)]
    for n in range(3):
        keep = lax.dynamic_index_in_dim(part, bits[n], 2 - n, keepdims=False)
        send = lax.dynamic_index_in_dim(part, 1 - bits[n], 2 - n, keepdims=False)
        part = keep + toggled(send, "section", 1 << n, SECTIONS)
    rows = unit_rows(part).astype(jnp.bfloat16)
    for n in (2, 1, 0):
        rows = jnp.stack([rows, toggled(rows, "section", 1 << n, SECTIONS)], axis=2 - n)
    for n in range(3):
        rows = jnp.where(bits[n] == 1, jnp.flip(rows, 2 - n), rows)
    return rows.reshape(SECTIONS, -1, width)


def body(acts, attn_proj, modulation, q_gain, text_feat, text_proj, text_len, kv_index, kv_count):
    acts, weights, modulation = acts[0], attn_proj[0], modulation[0]
    sequences, tokens, width = acts.shape
    yh, z, core = (lax.axis_index(name) for name in SEQ)
    member = 2 * yh + core
    place = jnp.stack([yh, z, core]).astype(jnp.int32)

    onward = [(i, (i + 1) % SECTIONS) for i in range(SECTIONS)]
    earlier = lax.ppermute(acts, "section", onward)
    packed = jnp.concatenate([modulation[:, 2], weights[3]])
    packed = lax.ppermute(packed, "section", onward)
    gate = packed[:sequences].astype(jnp.float32)[:, None, :]
    outer = packed[sequences:]

    modulated = modulate(acts, modulation)
    own = lax.all_to_all(modulated, "z", split_axis=0, concat_axis=0, tiled=True)
    own = own.reshape(-1, width)

    mine = []
    for other in range(MEMBERS):
        start = jnp.bitwise_xor(member, other) * COLS
        columns = [lax.dynamic_slice_in_dim(weights[kind], start, COLS, 1) for kind in range(3)]
        columns = jnp.concatenate(columns, axis=1)
        columns = toggled(columns, ("yh", "core"), other, MEMBERS) if other else columns
        mine.append(
            jnp.concatenate([columns, outer[:, other * COLS : (other + 1) * COLS]], axis=1)
        )
    mine = jnp.stack(mine)

    text = text_rows(text_feat, text_proj)
    own, text = hold([own, text], [mine, earlier])
    text = lax.all_to_all(text, "z", split_axis=0, concat_axis=0, tiled=True)
    own = jnp.concatenate([own, text.reshape(-1, width)])
    across = swap(own, "yh")
    (mine,) = hold([mine], [own], 10**11)
    right = left = mine
    blocks = [mine]
    for _ in range(3):
        right, left = moved(right, 1), moved(left, -1)
        blocks += [right, left]
    right, left = moved(right[:2], 1), moved(left[2:], -1)
    blocks += [right, left]
    (across,) = hold([across], [right, left])
    near, far = swap(own, "core"), swap(across, "core")

    pieces = pack(blocks)
    pieces_across, pieces_near = swap(pieces, "yh"), swap(pieces, "core")
    gain = lax.dynamic_slice_in_dim(q_gain, member * COLS, COLS, 1)
    parts = (own, near, across, far)
    made = layer(place, kv_index, kv_count, text_len, parts, blocks, gain)
    made = hold(made, [pieces_across, pieces_near])
    pieces = (pieces, pieces_near, pieces_across, swap(pieces_across, "core"))

    own_heads, other_heads = [], []
    for distance, block in zip(ORDER, made):
        route = [
            (s * RING + i, (s + 1) % SECTIONS * RING + (i + distance) % RING)
            for s in range(SECTIONS)
            for i in range(RING)
        ]
        own_heads.append(lax.ppermute(block, ("section", "z"), route))
    for half in range(2):
        for other in range(1, MEMBERS):
            block = jnp.stack([one[other] for one in own_heads[half * 4 : half * 4 + 4]])
            other_heads.append(toggled(block, ("yh", "core"), other, MEMBERS))
    fresh = finish(place, own_heads, other_heads, pieces, earlier, gate)
    return fresh[None]


def solution(mesh):
    fine = Mesh(mesh.devices.reshape(SECTIONS, 2, RING, 2), ("section",) + SEQ)
    in_specs = (
        P("section", None, SEQ, None),
        P("section", None, SEQ, None),
        P("section", None, None, None),
        P("section", None),
        P(None, SEQ, "section"),
        P("section", None),
        P(),
        P(),
        P(),
    )
    out_specs = P("section", None, SEQ, None)
    return jax.shard_map(body, mesh=fine, in_specs=in_specs, out_specs=out_specs, check_vma=False)
```

```python
import math

import jax
import jax.numpy as jnp
from jax import lax
from jax.experimental import pallas as pl
from jax.experimental.pallas import tpu as pltpu
from jax.sharding import Mesh
from jax.sharding import PartitionSpec as P

HEADS = 12
HEAD_DIM = 128
MEMBERS = 4
PER = HEADS // MEMBERS
COLS = PER * HEAD_DIM
SECTIONS = 8
RING = 8
SEQ = ("yh", "z", "core")
NEG = -1e30
ROOM = 60 * 2**20
VMEM = pl.BlockSpec(memory_space=pltpu.VMEM)
SMEM = pl.BlockSpec(memory_space=pltpu.SMEM)
ORDER = (4, 5, 0, 1, 3, 6, 2, 7)
RING_ORDER = (0, -1, 1, -2, 2, -3, 3, 4)


def unit_rows(values):
    return values * lax.rsqrt(jnp.mean(values * values, axis=-1, keepdims=True) + 1e-06)


def flip(bit, other):
    return bit + other - 2 * bit * other


def modulate_kernel(acts, modulation, out):
    shifts = modulation[0].astype(jnp.float32)
    scales = 1.0 + modulation[1].astype(jnp.float32)
    for at in range(acts.shape[0]):
        inputs = acts[at].astype(jnp.float32)
        mean = jnp.mean(inputs, axis=-1, keepdims=True)
        centred = inputs - mean
        variance = jnp.mean(centred * centred, axis=-1, keepdims=True)
        scaled = centred * lax.rsqrt(variance + 1e-06) * scales[at : at + 1]
        out[at] = (scaled + shifts[at : at + 1]).astype(jnp.bfloat16)


def modulate(acts, modulation):
    return pl.pallas_call(
        modulate_kernel,
        out_shape=jax.ShapeDtypeStruct(acts.shape, acts.dtype),
        in_specs=[VMEM, VMEM],
        out_specs=VMEM,
        compiler_params=pltpu.CompilerParams(vmem_limit_bytes=ROOM),
        cost_estimate=pl.CostEstimate(
            flops=10**11, bytes_accessed=4 * acts.size, transcendentals=0
        ),
        name="modulate",
    )(acts, modulation)


def hold_kernel(*refs):
    del refs


def hold(arrays, earlier=(), flops=0):
    hbm = pl.BlockSpec(memory_space=pl.ANY)
    return pl.pallas_call(
        hold_kernel,
        out_shape=[jax.ShapeDtypeStruct(one.shape, one.dtype) for one in arrays],
        in_specs=[hbm] * (len(arrays) + len(earlier)),
        out_specs=[hbm] * len(arrays),
        input_output_aliases={at: at for at in range(len(arrays))},
        compiler_params=pltpu.CompilerParams(vmem_limit_bytes=ROOM),
        cost_estimate=pl.CostEstimate(flops=flops, bytes_accessed=0, transcendentals=0),
        name="hold",
    )(*arrays, *earlier)


def layer_kernel(place, kv_index, kv_count, text_len, *refs):
    parts, blocks, gain, refs = refs[:4], refs[4:13], refs[13], refs[14:]
    outs, refs = refs[:8], refs[8:]
    xs, ws, ts, q, k, v, kc, vc, res, w_sem, t_sem, x_sem, out_sem = refs
    yh, z, core = place[0], place[1], place[2]
    rows = blocks[0].shape[1]
    tile, txt = q.shape[1], ts.shape[0]

    def lay(block, members, offset):
        source = lax.rem(z + offset + RING, RING)
        for at, member in enumerate(members):
            source_yh = flip(yh, member // 2)
            source_core = flip(core, member % 2)
            start = pl.multiple_of((source_yh * 16 + source * 2 + source_core) * rows, 16)
            pltpu.make_async_copy(
                block.at[at, :, : 3 * COLS], ws.at[pl.ds(start, rows)], w_sem
            ).start()

    for block, offset in zip(blocks[:7], RING_ORDER):
        lay(block, range(4), offset)
    lay(blocks[7], (0, 1), 4)
    lay(blocks[8], (2, 3), 4)
    own, quarter = xs.shape[1], txt // 4
    loads = [
        pltpu.make_async_copy(one.at[:own], xs.at[at], x_sem.at[at])
        for at, one in enumerate(parts)
    ]
    text_loads = [
        pltpu.make_async_copy(
            one.at[own:], ts.at[at * quarter : (at + 1) * quarter], t_sem.at[at]
        )
        for at, one in enumerate(parts)
    ]
    for load in loads + text_loads:
        load.start()
    pltpu.make_async_copy(ws, ws, w_sem).wait()

    for part, load in enumerate(loads):
        load.wait()
        made = jnp.dot(xs[part], ws[...], preferred_element_type=jnp.float32)
        slots = slice(part // 2 * 8, part // 2 * 8 + 8)
        half = slice(part % 2 * (tile // 2), (part % 2 + 1) * (tile // 2))
        for kind, out in enumerate((q, k, v)):
            for head in range(PER):
                lanes = slice(head * HEAD_DIM, (head + 1) * HEAD_DIM)
                first = kind * COLS + head * HEAD_DIM
                mine = made[:, first : first + HEAD_DIM]
                if kind < 2:
                    mine = unit_rows(mine)
                if kind == 0:
                    mine = mine * gain[:, lanes]
                out[slots, half, lanes] = mine.astype(jnp.bfloat16).reshape(
                    8, tile // 2, HEAD_DIM
                )

    for load in text_loads:
        load.wait()
    pair = jnp.dot(ts[...], ws[:, COLS:], preferred_element_type=jnp.float32)
    for head in range(PER):
        lanes = slice(head * HEAD_DIM, (head + 1) * HEAD_DIM)
        kc[:txt, lanes] = unit_rows(pair[:, lanes]).astype(jnp.bfloat16)
    vc[:txt, :] = pair[:, COLS:].astype(jnp.bfloat16)

    scale = math.log2(math.e) / math.sqrt(HEAD_DIM)
    row = lax.broadcasted_iota(jnp.int32, (1, txt), 1)
    row_yh = flip(row // 128, yh)
    row_core = flip((row // 64) % 2, core)
    token = (row_yh * 16 + ((row // 8) % 8) * 2 + row_core) * 8 + row % 8
    bias = jnp.where(token < text_len[z], 0.0, NEG)
    contract = (((1,), (1,)), ((), ()))
    sends = [
        pltpu.make_async_copy(res.at[at], out, out_sem.at[at]) for at, out in enumerate(outs)
    ]

    def one_tile(step, carry):
        at, ry = step // 2, step % 2
        home = lax.rem(z + place[3 + at], RING)
        slot = ry * 8 + home
        index = flip(yh, ry) * 8 + home
        count = kv_count[index]
        for c in range(4):

            @pl.when(c < count)
            def _(c=c):
                near = lax.rem(kv_index[index, c] + 8 * yh, 16)
                here = slice(txt + c * tile, txt + (c + 1) * tile)
                kc[here, :] = k[near]
                vc[here, :] = v[near]

        for n in range(1, 5):

            @pl.when(count == n)
            def _(n=n):
                size = txt + n * tile
                heads = [slice(head * HEAD_DIM, (head + 1) * HEAD_DIM) for head in range(PER)]
                scores = [
                    lax.dot_general(
                        q[slot, :, lanes],
                        kc[:size, lanes],
                        contract,
                        preferred_element_type=jnp.float32,
                    )
                    for lanes in heads
                ]
                scores = [
                    jnp.concatenate([one[:, :txt] * scale + bias, one[:, txt:] * scale], axis=1)
                    for one in scores
                ]
                tops = [jnp.max(one, axis=-1, keepdims=True) for one in scores]
                exps = [jnp.exp2(one - top) for one, top in zip(scores, tops)]
                inverses = [1.0 / jnp.sum(one, axis=-1, keepdims=True) for one in exps]
                probs = [
                    (one * inverse).astype(jnp.bfloat16) for one, inverse in zip(exps, inverses)
                ]
                mixed = [
                    jnp.dot(one, vc[:size, lanes], preferred_element_type=jnp.float32)
                    for one, lanes in zip(probs, heads)
                ]
                for one, lanes in zip(mixed, heads):
                    one = one.astype(jnp.bfloat16)
                    res[at, 2 * ry, :, lanes] = one[: tile // 2]
                    res[at, 2 * ry + 1, :, lanes] = one[tile // 2 :]

        for which, send in enumerate(sends):

            @pl.when(step == 2 * which + 1)
            def _(send=send):
                send.start()

        return carry

    lax.fori_loop(0, 16, one_tile, 0)
    for send in sends:
        send.wait()


def layer(place, kv_index, kv_count, text_len, parts, blocks, gain):
    width = parts[0].shape[1]
    rows = 512
    txt = 4 * (parts[0].shape[0] - rows)
    tile = 128
    hbm = pl.BlockSpec(memory_space=pl.ANY)
    order = jnp.array(ORDER, jnp.int32)
    out = jax.ShapeDtypeStruct((MEMBERS, tile // 2, COLS), jnp.bfloat16)
    heads = pltpu.VMEM((16, tile, COLS), jnp.bfloat16)
    near = pltpu.VMEM((txt + 4 * tile, COLS), jnp.bfloat16)
    return pl.pallas_call(
        layer_kernel,
        out_shape=(out,) * 8,
        in_specs=[SMEM] * 4 + [hbm] * 13 + [VMEM],
        out_specs=(hbm,) * 8,
        scratch_shapes=[
            pltpu.VMEM((4, rows, width), jnp.bfloat16),
            pltpu.VMEM((width, 3 * COLS), jnp.bfloat16),
            pltpu.VMEM((txt, width), jnp.bfloat16),
            heads,
            heads,
            heads,
            near,
            near,
            pltpu.VMEM((8, MEMBERS, tile // 2, COLS), jnp.bfloat16),
            pltpu.SemaphoreType.DMA,
            pltpu.SemaphoreType.DMA((4,)),
            pltpu.SemaphoreType.DMA((4,)),
            pltpu.SemaphoreType.DMA((8,)),
        ],
        compiler_params=pltpu.CompilerParams(vmem_limit_bytes=ROOM),
        cost_estimate=pl.CostEstimate(
            flops=5 * 10**10, bytes_accessed=14 * 2**20, transcendentals=5 * 10**6
        ),
        name="layer",
    )(jnp.concatenate([place, order]), kv_index, kv_count, text_len, *parts, *blocks, gain)


def finish_kernel(place, *refs):
    own, others = refs[:8], refs[8:14]
    pieces, refs = refs[14:18], refs[18:]
    acts_from, gate, out, xs, wo, acts, x_sem, wo_sem, acts_sem = refs
    yh, z, core = place[0], place[1], place[2]
    rows = pieces[0].shape[2]
    for other, block in enumerate(pieces):
        for slot, offset in enumerate(RING_ORDER):
            source = lax.rem(z + offset + RING, RING)
            source_yh = flip(yh, other // 2)
            source_core = flip(core, other % 2)
            start = pl.multiple_of((source_yh * 16 + source * 2 + source_core) * rows, 16)
            for group in range(4):
                lanes = slice(group * COLS, (group + 1) * COLS)
                pltpu.make_async_copy(
                    block.at[slot, group], wo.at[pl.ds(start, rows), lanes], wo_sem
                ).start()
    for other in range(MEMBERS):
        heads = flip(yh, other // 2) * 2 + flip(core, other % 2)
        lanes = pl.ds(pl.multiple_of(heads * COLS, 128), COLS)
        for at in range(8):
            if other == 0:
                block = own[at].at[0]
            else:
                block = others[(at // 4) * 3 + other - 1].at[at % 4]
            pltpu.make_async_copy(block, xs.at[pl.ds(at * 64, 64), lanes], x_sem).start()
    pltpu.make_async_copy(acts_from, acts, acts_sem).start()
    pltpu.make_async_copy(xs, xs, x_sem).wait()
    pltpu.make_async_copy(wo, wo, wo_sem).wait()
    pltpu.make_async_copy(acts_from, acts, acts_sem).wait()
    width = wo.shape[1]
    chunk = width // 3
    for piece in range(3):
        lanes = slice(piece * chunk, (piece + 1) * chunk)
        made = jnp.dot(xs[...], wo[:, lanes], preferred_element_type=jnp.float32)
        for at, distance in enumerate(ORDER):
            sequence = lax.rem(z - distance + RING, RING)
            out[sequence, :, lanes] = (
                acts[sequence, :, lanes].astype(jnp.float32)
                + gate[sequence, :, lanes] * made[at * 64 : (at + 1) * 64]
            ).astype(jnp.bfloat16)


def finish(place, own, others, pieces, acts, gate):
    width = acts.shape[2]
    hbm = pl.BlockSpec(memory_space=pl.ANY)
    return pl.pallas_call(
        finish_kernel,
        out_shape=jax.ShapeDtypeStruct(acts.shape, jnp.bfloat16),
        in_specs=[SMEM] + [hbm] * 19 + [VMEM],
        out_specs=VMEM,
        scratch_shapes=[
            pltpu.VMEM((512, width), jnp.bfloat16),
            pltpu.VMEM((width, width), jnp.bfloat16),
            pltpu.VMEM(acts.shape, jnp.bfloat16),
            pltpu.SemaphoreType.DMA,
            pltpu.SemaphoreType.DMA,
            pltpu.SemaphoreType.DMA,
        ],
        compiler_params=pltpu.CompilerParams(vmem_limit_bytes=ROOM),
        cost_estimate=pl.CostEstimate(
            flops=2 * 512 * 1536 * 1536, bytes_accessed=12 * 2**20, transcendentals=0
        ),
        name="finish",
    )(place, *own, *others, *pieces, acts, gate)


def swap(block, axis):
    return lax.ppermute(block, axis, [(0, 1), (1, 0)])


def toggled(block, axis, bits, size):
    return lax.ppermute(block, axis, [(i, i ^ bits) for i in range(size)])


def moved(block, distance):
    return lax.ppermute(block, "z", [(i, (i + distance) % RING) for i in range(RING)])


def text_rows(text_feat, text_proj):
    section = lax.axis_index("section")
    width = text_proj.shape[1]
    part = jnp.dot(
        text_feat.reshape(-1, text_feat.shape[2]), text_proj, preferred_element_type=jnp.float32
    ).reshape(2, 2, 2, -1, width)
    bits = [(section >> n) & 1 for n in range(3)]
    for n in range(3):
        keep = lax.dynamic_index_in_dim(part, bits[n], 2 - n, keepdims=False)
        send = lax.dynamic_index_in_dim(part, 1 - bits[n], 2 - n, keepdims=False)
        part = keep + toggled(send, "section", 1 << n, SECTIONS)
    rows = unit_rows(part).astype(jnp.bfloat16)
    for n in (2, 1, 0):
        rows = jnp.stack([rows, toggled(rows, "section", 1 << n, SECTIONS)], axis=2 - n)
    for n in range(3):
        rows = jnp.where(bits[n] == 1, jnp.flip(rows, 2 - n), rows)
    return rows.reshape(SECTIONS, -1, width)


def body(acts, attn_proj, modulation, q_gain, text_feat, text_proj, text_len, kv_index, kv_count):
    acts, weights, modulation = acts[0], attn_proj[0], modulation[0]
    sequences, tokens, width = acts.shape
    yh, z, core = (lax.axis_index(name) for name in SEQ)
    member = 2 * yh + core
    place = jnp.stack([yh, z, core]).astype(jnp.int32)

    onward = [(i, (i + 1) % SECTIONS) for i in range(SECTIONS)]
    earlier = lax.ppermute(acts, "section", onward)
    packed = jnp.concatenate([modulation[:, 2], weights[3]])
    packed = lax.ppermute(packed, "section", onward)
    gate = packed[:sequences].astype(jnp.float32)[:, None, :]
    outer = packed[sequences:]

    modulated = modulate(acts, modulation.transpose(1, 0, 2))
    own = lax.all_to_all(modulated, "z", split_axis=0, concat_axis=0, tiled=True)
    own = own.reshape(-1, width)

    mine = []
    for other in range(MEMBERS):
        start = jnp.bitwise_xor(member, other) * COLS
        columns = [lax.dynamic_slice_in_dim(weights[kind], start, COLS, 1) for kind in range(3)]
        columns = jnp.concatenate(columns, axis=1)
        columns = toggled(columns, ("yh", "core"), other, MEMBERS) if other else columns
        mine.append(
            jnp.concatenate([columns, outer[:, other * COLS : (other + 1) * COLS]], axis=1)
        )
    mine = jnp.stack(mine)

    text = text_rows(text_feat, text_proj)
    own, text, mine = hold([own, text, mine])
    right, left = moved(mine, 1), moved(mine, -1)
    (text,) = hold([text], [own, mine], 10**11)
    text = lax.all_to_all(text, "z", split_axis=0, concat_axis=0, tiled=True)
    own = jnp.concatenate([own, text.reshape(-1, width)])
    across = swap(own, "yh")
    right, left = hold([right, left], [own], 10**11)
    blocks = [mine, right, left]
    for _ in range(2):
        right, left = moved(right, 1), moved(left, -1)
        blocks += [right, left]
    right, left = moved(right[:2], 1), moved(left[2:], -1)
    blocks += [right, left]
    last = jnp.concatenate([right, left])
    pieces = jnp.stack([one[:, :, 3 * COLS :] for one in (*blocks[:7], last)])
    (across,) = hold([across], [right, left])
    near, far = swap(own, "core"), swap(across, "core")

    pieces_across, pieces_near = swap(pieces, "yh"), swap(pieces, "core")
    gain = lax.dynamic_slice_in_dim(q_gain, member * COLS, COLS, 1)
    parts = (own, near, across, far)
    made = layer(place, kv_index, kv_count, text_len, parts, blocks, gain)
    made = (*hold(made[:4], [pieces_across, pieces_near]), *hold(made[4:], [earlier]))
    pieces = (pieces, pieces_near, pieces_across, swap(pieces_across, "core"))

    own_heads, other_heads = [], []
    for distance, block in zip(ORDER, made):
        route = [
            (s * RING + i, (s + 1) % SECTIONS * RING + (i + distance) % RING)
            for s in range(SECTIONS)
            for i in range(RING)
        ]
        own_heads.append(lax.ppermute(block, ("section", "z"), route))
    for half in range(2):
        for other in range(1, MEMBERS):
            block = jnp.stack([one[other] for one in own_heads[half * 4 : half * 4 + 4]])
            other_heads.append(toggled(block, ("yh", "core"), other, MEMBERS))
    fresh = finish(place, own_heads, other_heads, pieces, earlier, gate)
    return fresh[None]


def solution(mesh):
    fine = Mesh(mesh.devices.reshape(SECTIONS, 2, RING, 2), ("section",) + SEQ)
    in_specs = (
        P("section", None, SEQ, None),
        P("section", None, SEQ, None),
        P("section", None, None, None),
        P("section", None),
        P(None, SEQ, "section"),
        P("section", None),
        P(),
        P(),
        P(),
    )
    out_specs = P("section", None, SEQ, None)
    return jax.shard_map(body, mesh=fine, in_specs=in_specs, out_specs=out_specs, check_vma=False)
```

```python
import math

import jax
import jax.numpy as jnp
from jax import lax
from jax.experimental import pallas as pl
from jax.experimental.pallas import tpu as pltpu
from jax.sharding import Mesh
from jax.sharding import PartitionSpec as P

HEADS = 12
HEAD_DIM = 128
MEMBERS = 4
PER = HEADS // MEMBERS
COLS = PER * HEAD_DIM
SECTIONS = 8
RING = 8
SEQ = ("yh", "z", "core")
NEG = -1e30
ROOM = 60 * 2**20
VMEM = pl.BlockSpec(memory_space=pltpu.VMEM)
SMEM = pl.BlockSpec(memory_space=pltpu.SMEM)
ORDER = (4, 5, 0, 1, 3, 6, 2, 7)
RING_ORDER = (0, -1, 1, -2, 2, -3, 3, 4)


def unit_rows(values):
    return values * lax.rsqrt(jnp.mean(values * values, axis=-1, keepdims=True) + 1e-06)


def flip(bit, other):
    return bit + other - 2 * bit * other


def modulate_kernel(acts, modulation, out):
    shifts = modulation[0].astype(jnp.float32)
    scales = 1.0 + modulation[1].astype(jnp.float32)
    for at in range(acts.shape[0]):
        inputs = acts[at].astype(jnp.float32)
        mean = jnp.mean(inputs, axis=-1, keepdims=True)
        centred = inputs - mean
        variance = jnp.mean(centred * centred, axis=-1, keepdims=True)
        scaled = centred * lax.rsqrt(variance + 1e-06) * scales[at : at + 1]
        out[at] = (scaled + shifts[at : at + 1]).astype(jnp.bfloat16)


def modulate(acts, modulation):
    return pl.pallas_call(
        modulate_kernel,
        out_shape=jax.ShapeDtypeStruct(acts.shape, acts.dtype),
        in_specs=[VMEM, VMEM],
        out_specs=VMEM,
        compiler_params=pltpu.CompilerParams(vmem_limit_bytes=ROOM),
        cost_estimate=pl.CostEstimate(
            flops=10**11, bytes_accessed=4 * acts.size, transcendentals=0
        ),
        name="modulate",
    )(acts, modulation)


def hold_kernel(*refs):
    del refs


def hold(arrays, earlier=(), flops=0):
    hbm = pl.BlockSpec(memory_space=pl.ANY)
    return pl.pallas_call(
        hold_kernel,
        out_shape=[jax.ShapeDtypeStruct(one.shape, one.dtype) for one in arrays],
        in_specs=[hbm] * (len(arrays) + len(earlier)),
        out_specs=[hbm] * len(arrays),
        input_output_aliases={at: at for at in range(len(arrays))},
        compiler_params=pltpu.CompilerParams(vmem_limit_bytes=ROOM),
        cost_estimate=pl.CostEstimate(flops=flops, bytes_accessed=0, transcendentals=0),
        name="hold",
    )(*arrays, *earlier)


def layer_kernel(place, kv_index, kv_count, text_len, *refs):
    parts, blocks, gain, refs = refs[:4], refs[4:13], refs[13], refs[14:]
    outs, refs = refs[:8], refs[8:]
    xs, ws, ts, q, k, v, kc, vc, res, w_sem, t_sem, x_sem, out_sem = refs
    yh, z, core = place[0], place[1], place[2]
    rows = blocks[0].shape[1]
    tile, txt = q.shape[1], ts.shape[0]

    def lay(block, members, offset):
        source = lax.rem(z + offset + RING, RING)
        for at, member in enumerate(members):
            source_yh = flip(yh, member // 2)
            source_core = flip(core, member % 2)
            start = pl.multiple_of((source_yh * 16 + source * 2 + source_core) * rows, 16)
            pltpu.make_async_copy(
                block.at[at, :, : 3 * COLS], ws.at[pl.ds(start, rows)], w_sem
            ).start()

    for block, offset in zip(blocks[:7], RING_ORDER):
        lay(block, range(4), offset)
    lay(blocks[7], (0, 1), 4)
    lay(blocks[8], (2, 3), 4)
    own, quarter = xs.shape[1], txt // 4
    loads = [
        pltpu.make_async_copy(one.at[:own], xs.at[at], x_sem.at[at])
        for at, one in enumerate(parts)
    ]
    text_loads = [
        pltpu.make_async_copy(
            one.at[own:], ts.at[at * quarter : (at + 1) * quarter], t_sem.at[at]
        )
        for at, one in enumerate(parts)
    ]
    for load in loads + text_loads:
        load.start()
    pltpu.make_async_copy(ws, ws, w_sem).wait()

    for part, load in enumerate(loads):
        load.wait()
        made = jnp.dot(xs[part], ws[...], preferred_element_type=jnp.float32)
        slots = slice(part // 2 * 8, part // 2 * 8 + 8)
        half = slice(part % 2 * (tile // 2), (part % 2 + 1) * (tile // 2))
        for kind, out in enumerate((q, k, v)):
            for head in range(PER):
                lanes = slice(head * HEAD_DIM, (head + 1) * HEAD_DIM)
                first = kind * COLS + head * HEAD_DIM
                mine = made[:, first : first + HEAD_DIM]
                if kind < 2:
                    mine = unit_rows(mine)
                if kind == 0:
                    mine = mine * gain[:, lanes]
                out[slots, half, lanes] = mine.astype(jnp.bfloat16).reshape(
                    8, tile // 2, HEAD_DIM
                )

    for load in text_loads:
        load.wait()
    pair = jnp.dot(ts[...], ws[:, COLS:], preferred_element_type=jnp.float32)
    for head in range(PER):
        lanes = slice(head * HEAD_DIM, (head + 1) * HEAD_DIM)
        kc[:txt, lanes] = unit_rows(pair[:, lanes]).astype(jnp.bfloat16)
    vc[:txt, :] = pair[:, COLS:].astype(jnp.bfloat16)

    scale = math.log2(math.e) / math.sqrt(HEAD_DIM)
    row = lax.broadcasted_iota(jnp.int32, (1, txt), 1)
    row_yh = flip(row // 128, yh)
    row_core = flip((row // 64) % 2, core)
    token = (row_yh * 16 + ((row // 8) % 8) * 2 + row_core) * 8 + row % 8
    bias = jnp.where(token < text_len[z], 0.0, NEG)
    contract = (((1,), (1,)), ((), ()))
    sends = [
        pltpu.make_async_copy(res.at[at], out, out_sem.at[at]) for at, out in enumerate(outs)
    ]

    def one_tile(step, carry):
        at, ry = step // 2, step % 2
        home = lax.rem(z + place[3 + at], RING)
        slot = ry * 8 + home
        index = flip(yh, ry) * 8 + home
        count = kv_count[index]
        for c in range(4):

            @pl.when(c < count)
            def _(c=c):
                near = lax.rem(kv_index[index, c] + 8 * yh, 16)
                here = slice(txt + c * tile, txt + (c + 1) * tile)
                kc[here, :] = k[near]
                vc[here, :] = v[near]

        for n in range(1, 5):

            @pl.when(count == n)
            def _(n=n):
                size = txt + n * tile
                heads = [slice(head * HEAD_DIM, (head + 1) * HEAD_DIM) for head in range(PER)]
                scores = [
                    lax.dot_general(
                        q[slot, :, lanes],
                        kc[:size, lanes],
                        contract,
                        preferred_element_type=jnp.float32,
                    )
                    for lanes in heads
                ]
                scores = [
                    jnp.concatenate([one[:, :txt] * scale + bias, one[:, txt:] * scale], axis=1)
                    for one in scores
                ]
                tops = [jnp.max(one, axis=-1, keepdims=True) for one in scores]
                exps = [jnp.exp2(one - top) for one, top in zip(scores, tops)]
                inverses = [1.0 / jnp.sum(one, axis=-1, keepdims=True) for one in exps]
                probs = [
                    (one * inverse).astype(jnp.bfloat16) for one, inverse in zip(exps, inverses)
                ]
                mixed = [
                    jnp.dot(one, vc[:size, lanes], preferred_element_type=jnp.float32)
                    for one, lanes in zip(probs, heads)
                ]
                for one, lanes in zip(mixed, heads):
                    one = one.astype(jnp.bfloat16)
                    res[at, 2 * ry, :, lanes] = one[: tile // 2]
                    res[at, 2 * ry + 1, :, lanes] = one[tile // 2 :]

        for which, send in enumerate(sends):

            @pl.when(step == 2 * which + 1)
            def _(send=send):
                send.start()

        return carry

    lax.fori_loop(0, 16, one_tile, 0)
    for send in sends:
        send.wait()


def layer(place, kv_index, kv_count, text_len, parts, blocks, gain):
    width = parts[0].shape[1]
    rows = 512
    txt = 4 * (parts[0].shape[0] - rows)
    tile = 128
    hbm = pl.BlockSpec(memory_space=pl.ANY)
    order = jnp.array(ORDER, jnp.int32)
    out = jax.ShapeDtypeStruct((MEMBERS, tile // 2, COLS), jnp.bfloat16)
    heads = pltpu.VMEM((16, tile, COLS), jnp.bfloat16)
    near = pltpu.VMEM((txt + 4 * tile, COLS), jnp.bfloat16)
    return pl.pallas_call(
        layer_kernel,
        out_shape=(out,) * 8,
        in_specs=[SMEM] * 4 + [hbm] * 13 + [VMEM],
        out_specs=(hbm,) * 8,
        scratch_shapes=[
            pltpu.VMEM((4, rows, width), jnp.bfloat16),
            pltpu.VMEM((width, 3 * COLS), jnp.bfloat16),
            pltpu.VMEM((txt, width), jnp.bfloat16),
            heads,
            heads,
            heads,
            near,
            near,
            pltpu.VMEM((8, MEMBERS, tile // 2, COLS), jnp.bfloat16),
            pltpu.SemaphoreType.DMA,
            pltpu.SemaphoreType.DMA((4,)),
            pltpu.SemaphoreType.DMA((4,)),
            pltpu.SemaphoreType.DMA((8,)),
        ],
        compiler_params=pltpu.CompilerParams(vmem_limit_bytes=ROOM),
        cost_estimate=pl.CostEstimate(
            flops=5 * 10**10, bytes_accessed=14 * 2**20, transcendentals=5 * 10**6
        ),
        name="layer",
    )(jnp.concatenate([place, order]), kv_index, kv_count, text_len, *parts, *blocks, gain)


def pack_kernel(*refs):
    blocks, out, sem = refs[:9], refs[9], refs[10]

    def lay(block, group, slot, to):
        lanes = slice(to * COLS, (to + 1) * COLS)
        pltpu.make_async_copy(block.at[group, :, 3 * COLS :], out.at[slot, :, lanes], sem).start()

    for slot, block in enumerate(blocks[:7]):
        for group in range(4):
            lay(block, group, slot, group)
    for group in range(4):
        lay(blocks[7 + group // 2], group % 2, 7, group)
    pltpu.make_async_copy(out, out, sem).wait()


def pack(blocks):
    _, rows, width = blocks[0].shape
    return pl.pallas_call(
        pack_kernel,
        out_shape=jax.ShapeDtypeStruct((RING, rows, width), jnp.bfloat16),
        in_specs=[pl.BlockSpec(memory_space=pl.ANY)] * 9,
        out_specs=VMEM,
        scratch_shapes=[pltpu.SemaphoreType.DMA],
        compiler_params=pltpu.CompilerParams(vmem_limit_bytes=ROOM),
        cost_estimate=pl.CostEstimate(flops=0, bytes_accessed=2 * 2**20, transcendentals=0),
        name="pack",
    )(*blocks)


def finish_kernel(place, *refs):
    own, others = refs[:8], refs[8:14]
    pieces, refs = refs[14:18], refs[18:]
    acts_from, gate, out, xs, wo, acts, x_sem, wo_sem, acts_sem = refs
    yh, z, core = place[0], place[1], place[2]
    rows = pieces[0].shape[1]
    for other, block in enumerate(pieces):
        for slot, offset in enumerate(RING_ORDER):
            source = lax.rem(z + offset + RING, RING)
            source_yh = flip(yh, other // 2)
            source_core = flip(core, other % 2)
            start = pl.multiple_of((source_yh * 16 + source * 2 + source_core) * rows, 16)
            pltpu.make_async_copy(block.at[slot], wo.at[pl.ds(start, rows)], wo_sem).start()
    for other in range(MEMBERS):
        heads = flip(yh, other // 2) * 2 + flip(core, other % 2)
        lanes = pl.ds(pl.multiple_of(heads * COLS, 128), COLS)
        if other == 0:
            for at in range(8):
                pltpu.make_async_copy(own[at].at[0], xs.at[at, :, lanes], x_sem).start()
        else:
            for part in range(2):
                block = others[part * 3 + other - 1]
                here = slice(part * 4, part * 4 + 4)
                pltpu.make_async_copy(block, xs.at[here, :, lanes], x_sem).start()
    pltpu.make_async_copy(acts_from, acts, acts_sem).start()
    pltpu.make_async_copy(xs, xs, x_sem).wait()
    pltpu.make_async_copy(wo, wo, wo_sem).wait()
    pltpu.make_async_copy(acts_from, acts, acts_sem).wait()
    width = wo.shape[1]
    chunk = width // 3
    for piece in range(3):
        lanes = slice(piece * chunk, (piece + 1) * chunk)
        made = jnp.dot(
            xs[...].reshape(512, width), wo[:, lanes], preferred_element_type=jnp.float32
        )
        for at, distance in enumerate(ORDER):
            sequence = lax.rem(z - distance + RING, RING)
            out[sequence, :, lanes] = (
                acts[sequence, :, lanes].astype(jnp.float32)
                + gate[sequence, :, lanes] * made[at * 64 : (at + 1) * 64]
            ).astype(jnp.bfloat16)


def finish(place, own, others, pieces, acts, gate):
    width = acts.shape[2]
    hbm = pl.BlockSpec(memory_space=pl.ANY)
    return pl.pallas_call(
        finish_kernel,
        out_shape=jax.ShapeDtypeStruct(acts.shape, jnp.bfloat16),
        in_specs=[SMEM] + [hbm] * 19 + [VMEM],
        out_specs=VMEM,
        scratch_shapes=[
            pltpu.VMEM((8, 64, width), jnp.bfloat16),
            pltpu.VMEM((width, width), jnp.bfloat16),
            pltpu.VMEM(acts.shape, jnp.bfloat16),
            pltpu.SemaphoreType.DMA,
            pltpu.SemaphoreType.DMA,
            pltpu.SemaphoreType.DMA,
        ],
        compiler_params=pltpu.CompilerParams(vmem_limit_bytes=ROOM),
        cost_estimate=pl.CostEstimate(
            flops=2 * 512 * 1536 * 1536, bytes_accessed=12 * 2**20, transcendentals=0
        ),
        name="finish",
    )(place, *own, *others, *pieces, acts, gate)


def swap(block, axis):
    return lax.ppermute(block, axis, [(0, 1), (1, 0)])


def toggled(block, axis, bits, size):
    return lax.ppermute(block, axis, [(i, i ^ bits) for i in range(size)])


def moved(block, distance):
    return lax.ppermute(block, "z", [(i, (i + distance) % RING) for i in range(RING)])


def text_rows(text_feat, text_proj):
    section = lax.axis_index("section")
    width = text_proj.shape[1]
    part = jnp.dot(
        text_feat.reshape(-1, text_feat.shape[2]), text_proj, preferred_element_type=jnp.float32
    ).reshape(2, 2, 2, -1, width)
    bits = [(section >> n) & 1 for n in range(3)]
    for n in range(3):
        keep = lax.dynamic_index_in_dim(part, bits[n], 2 - n, keepdims=False)
        send = lax.dynamic_index_in_dim(part, 1 - bits[n], 2 - n, keepdims=False)
        part = keep + toggled(send, "section", 1 << n, SECTIONS)
    rows = unit_rows(part).astype(jnp.bfloat16)
    for n in (2, 1, 0):
        rows = jnp.stack([rows, toggled(rows, "section", 1 << n, SECTIONS)], axis=2 - n)
    for n in range(3):
        rows = jnp.where(bits[n] == 1, jnp.flip(rows, 2 - n), rows)
    return rows.reshape(SECTIONS, -1, width)


def body(acts, attn_proj, modulation, q_gain, text_feat, text_proj, text_len, kv_index, kv_count):
    acts, weights, modulation = acts[0], attn_proj[0], modulation[0]
    sequences, tokens, width = acts.shape
    yh, z, core = (lax.axis_index(name) for name in SEQ)
    member = 2 * yh + core
    place = jnp.stack([yh, z, core]).astype(jnp.int32)

    onward = [(i, (i + 1) % SECTIONS) for i in range(SECTIONS)]
    earlier = lax.ppermute(acts, "section", onward)
    packed = jnp.concatenate([modulation[:, 2], weights[3]])
    packed = lax.ppermute(packed, "section", onward)
    gate = packed[:sequences].astype(jnp.float32)[:, None, :]
    outer = packed[sequences:]

    modulated = modulate(acts, modulation.transpose(1, 0, 2))
    own = lax.all_to_all(modulated, "z", split_axis=0, concat_axis=0, tiled=True)
    own = own.reshape(-1, width)

    mine = []
    for other in range(MEMBERS):
        start = jnp.bitwise_xor(member, other) * COLS
        columns = [lax.dynamic_slice_in_dim(weights[kind], start, COLS, 1) for kind in range(3)]
        columns = jnp.concatenate(columns, axis=1)
        columns = toggled(columns, ("yh", "core"), other, MEMBERS) if other else columns
        mine.append(
            jnp.concatenate([columns, outer[:, other * COLS : (other + 1) * COLS]], axis=1)
        )
    mine = jnp.stack(mine)

    text = text_rows(text_feat, text_proj)
    own, text, mine = hold([own, text, mine])
    right, left = moved(mine, 1), moved(mine, -1)
    (text,) = hold([text], [own, mine], 10**11)
    text = lax.all_to_all(text, "z", split_axis=0, concat_axis=0, tiled=True)
    own = jnp.concatenate([own, text.reshape(-1, width)])
    across = swap(own, "yh")
    right, left = hold([right, left], [own], 10**11)
    blocks = [mine, right, left]
    for _ in range(2):
        right, left = moved(right, 1), moved(left, -1)
        blocks += [right, left]
    right, left = moved(right[:2], 1), moved(left[2:], -1)
    blocks += [right, left]
    (across,) = hold([across], [right, left])
    near, far = swap(own, "core"), swap(across, "core")

    pieces = pack(blocks)
    pieces_across, pieces_near = swap(pieces, "yh"), swap(pieces, "core")
    gain = lax.dynamic_slice_in_dim(q_gain, member * COLS, COLS, 1)
    parts = (own, near, across, far)
    made = layer(place, kv_index, kv_count, text_len, parts, blocks, gain)
    made = (*hold(made[:4], [pieces_across, pieces_near]), *made[4:])
    pieces_far = swap(pieces_across, "core")
    pieces = (pieces, pieces_near, pieces_across, pieces_far)

    def go_home(block, distance):
        route = [
            (s * RING + i, (s + 1) % SECTIONS * RING + (i + distance) % RING)
            for s in range(SECTIONS)
            for i in range(RING)
        ]
        return lax.ppermute(block, ("section", "z"), route)

    def to_swap(blocks):
        return [jnp.stack([one[other] for one in blocks]) for other in range(1, MEMBERS)]

    def exchange(blocks):
        return [
            toggled(block, ("yh", "core"), other + 1, MEMBERS) for other, block in enumerate(blocks)
        ]

    own_heads = [go_home(*one) for one in zip(made[:4], ORDER[:4])]
    middle = hold(made[4:6], [earlier, pieces_far])
    own_heads += [go_home(*one) for one in zip(middle, ORDER[4:6])]
    first = to_swap(own_heads[:4])
    final = hold(made[6:], [*first, middle[0]], 10**11)
    own_heads += [go_home(*one) for one in zip(final, ORDER[6:])]
    other_heads = exchange(first) + exchange(to_swap(own_heads[4:]))
    fresh = finish(place, own_heads, other_heads, pieces, earlier, gate)
    return fresh[None]


def solution(mesh):
    fine = Mesh(mesh.devices.reshape(SECTIONS, 2, RING, 2), ("section",) + SEQ)
    in_specs = (
        P("section", None, SEQ, None),
        P("section", None, SEQ, None),
        P("section", None, None, None),
        P("section", None),
        P(None, SEQ, "section"),
        P("section", None),
        P(),
        P(),
        P(),
    )
    out_specs = P("section", None, SEQ, None)
    return jax.shard_map(body, mesh=fine, in_specs=in_specs, out_specs=out_specs, check_vma=False)
```

```python
import math

import jax
import jax.numpy as jnp
from jax import lax
from jax.experimental import pallas as pl
from jax.experimental.pallas import tpu as pltpu
from jax.sharding import Mesh
from jax.sharding import PartitionSpec as P

HEADS = 12
HEAD_DIM = 128
MEMBERS = 4
PER = HEADS // MEMBERS
COLS = PER * HEAD_DIM
SECTIONS = 8
RING = 8
SEQ = ("yh", "z", "core")
NEG = -1e30
ROOM = 60 * 2**20
VMEM = pl.BlockSpec(memory_space=pltpu.VMEM)
SMEM = pl.BlockSpec(memory_space=pltpu.SMEM)
ORDER = (4, 5, 0, 1, 3, 6, 2, 7)
RING_ORDER = (0, -1, 1, -2, 2, -3, 3, 4)


def unit_rows(values):
    return values * lax.rsqrt(jnp.mean(values * values, axis=-1, keepdims=True) + 1e-06)


def flip(bit, other):
    return bit + other - 2 * bit * other


def modulate_kernel(acts, modulation, out):
    shifts = modulation[0].astype(jnp.float32)
    scales = 1.0 + modulation[1].astype(jnp.float32)
    for at in range(acts.shape[0]):
        inputs = acts[at].astype(jnp.float32)
        mean = jnp.mean(inputs, axis=-1, keepdims=True)
        centred = inputs - mean
        variance = jnp.mean(centred * centred, axis=-1, keepdims=True)
        scaled = centred * lax.rsqrt(variance + 1e-06) * scales[at : at + 1]
        out[at] = (scaled + shifts[at : at + 1]).astype(jnp.bfloat16)


def modulate(acts, modulation):
    return pl.pallas_call(
        modulate_kernel,
        out_shape=jax.ShapeDtypeStruct(acts.shape, acts.dtype),
        in_specs=[VMEM, VMEM],
        out_specs=VMEM,
        compiler_params=pltpu.CompilerParams(vmem_limit_bytes=ROOM),
        cost_estimate=pl.CostEstimate(
            flops=10**11, bytes_accessed=4 * acts.size, transcendentals=0
        ),
        name="modulate",
    )(acts, modulation)


def hold_kernel(*refs):
    del refs


def hold(arrays, earlier=(), flops=0):
    hbm = pl.BlockSpec(memory_space=pl.ANY)
    return pl.pallas_call(
        hold_kernel,
        out_shape=[jax.ShapeDtypeStruct(one.shape, one.dtype) for one in arrays],
        in_specs=[hbm] * (len(arrays) + len(earlier)),
        out_specs=[hbm] * len(arrays),
        input_output_aliases={at: at for at in range(len(arrays))},
        compiler_params=pltpu.CompilerParams(vmem_limit_bytes=ROOM),
        cost_estimate=pl.CostEstimate(flops=flops, bytes_accessed=0, transcendentals=0),
        name="hold",
    )(*arrays, *earlier)


def layer_kernel(place, kv_index, kv_count, text_len, *refs):
    parts, blocks, texts, gain, refs = refs[:4], refs[4:13], refs[13:17], refs[17], refs[18:]
    outs, refs = refs[:8], refs[8:]
    xs, ws, ts, q, k, v, kc, vc, res, w_sem, t_sem, x_sem, out_sem = refs
    yh, z, core = place[0], place[1], place[2]
    rows = blocks[0].shape[1]
    tile, txt = q.shape[1], ts.shape[0]

    def lay(block, members, offset):
        source = lax.rem(z + offset + RING, RING)
        for at, member in enumerate(members):
            source_yh = flip(yh, member // 2)
            source_core = flip(core, member % 2)
            start = pl.multiple_of((source_yh * 16 + source * 2 + source_core) * rows, 16)
            pltpu.make_async_copy(
                block.at[at, :, : 3 * COLS], ws.at[pl.ds(start, rows)], w_sem
            ).start()

    for block, offset in zip(blocks[:7], RING_ORDER):
        lay(block, range(4), offset)
    lay(blocks[7], (0, 1), 4)
    lay(blocks[8], (2, 3), 4)
    quarter = txt // 4
    loads = [pltpu.make_async_copy(one, xs.at[at], x_sem.at[at]) for at, one in enumerate(parts)]
    text_loads = [
        pltpu.make_async_copy(one, ts.at[at * quarter : (at + 1) * quarter], t_sem.at[at])
        for at, one in enumerate(texts)
    ]
    for load in loads + text_loads:
        load.start()
    pltpu.make_async_copy(ws, ws, w_sem).wait()

    for part, load in enumerate(loads):
        load.wait()
        made = jnp.dot(xs[part], ws[...], preferred_element_type=jnp.float32)
        slots = slice(part // 2 * 8, part // 2 * 8 + 8)
        half = slice(part % 2 * (tile // 2), (part % 2 + 1) * (tile // 2))
        for kind, out in enumerate((q, k, v)):
            for head in range(PER):
                lanes = slice(head * HEAD_DIM, (head + 1) * HEAD_DIM)
                first = kind * COLS + head * HEAD_DIM
                mine = made[:, first : first + HEAD_DIM]
                if kind < 2:
                    mine = unit_rows(mine)
                if kind == 0:
                    mine = mine * gain[:, lanes]
                out[slots, half, lanes] = mine.astype(jnp.bfloat16).reshape(
                    8, tile // 2, HEAD_DIM
                )

    for load in text_loads:
        load.wait()
    pair = jnp.dot(ts[...], ws[:, COLS:], preferred_element_type=jnp.float32)
    for head in range(PER):
        lanes = slice(head * HEAD_DIM, (head + 1) * HEAD_DIM)
        kc[:txt, lanes] = unit_rows(pair[:, lanes]).astype(jnp.bfloat16)
    vc[:txt, :] = pair[:, COLS:].astype(jnp.bfloat16)

    scale = math.log2(math.e) / math.sqrt(HEAD_DIM)
    row = lax.broadcasted_iota(jnp.int32, (1, txt), 1)
    row_yh = flip(row // 128, yh)
    row_core = flip((row // 64) % 2, core)
    token = (row_yh * 16 + ((row // 8) % 8) * 2 + row_core) * 8 + row % 8
    bias = jnp.where(token < text_len[z], 0.0, NEG)
    contract = (((1,), (1,)), ((), ()))
    sends = [
        pltpu.make_async_copy(res.at[at], out, out_sem.at[at]) for at, out in enumerate(outs)
    ]

    def one_tile(step, carry):
        at, ry = step // 2, step % 2
        home = lax.rem(z + place[3 + at], RING)
        slot = ry * 8 + home
        index = flip(yh, ry) * 8 + home
        count = kv_count[index]
        for c in range(4):

            @pl.when(c < count)
            def _(c=c):
                near = lax.rem(kv_index[index, c] + 8 * yh, 16)
                here = slice(txt + c * tile, txt + (c + 1) * tile)
                kc[here, :] = k[near]
                vc[here, :] = v[near]

        for n in range(1, 5):

            @pl.when(count == n)
            def _(n=n):
                size = txt + n * tile
                heads = [slice(head * HEAD_DIM, (head + 1) * HEAD_DIM) for head in range(PER)]
                scores = [
                    lax.dot_general(
                        q[slot, :, lanes],
                        kc[:size, lanes],
                        contract,
                        preferred_element_type=jnp.float32,
                    )
                    for lanes in heads
                ]
                scores = [
                    jnp.concatenate([one[:, :txt] * scale + bias, one[:, txt:] * scale], axis=1)
                    for one in scores
                ]
                tops = [jnp.max(one, axis=-1, keepdims=True) for one in scores]
                exps = [jnp.exp2(one - top) for one, top in zip(scores, tops)]
                inverses = [1.0 / jnp.sum(one, axis=-1, keepdims=True) for one in exps]
                probs = [
                    (one * inverse).astype(jnp.bfloat16) for one, inverse in zip(exps, inverses)
                ]
                mixed = [
                    jnp.dot(one, vc[:size, lanes], preferred_element_type=jnp.float32)
                    for one, lanes in zip(probs, heads)
                ]
                for one, lanes in zip(mixed, heads):
                    one = one.astype(jnp.bfloat16)
                    res[at, 2 * ry, :, lanes] = one[: tile // 2]
                    res[at, 2 * ry + 1, :, lanes] = one[tile // 2 :]

        for which, send in enumerate(sends):

            @pl.when(step == 2 * which + 1)
            def _(send=send):
                send.start()

        return carry

    lax.fori_loop(0, 16, one_tile, 0)
    for send in sends:
        send.wait()


def layer(place, kv_index, kv_count, text_len, parts, blocks, texts, gain):
    rows, width = parts[0].shape
    txt = 4 * texts[0].shape[0]
    tile = 128
    hbm = pl.BlockSpec(memory_space=pl.ANY)
    order = jnp.array(ORDER, jnp.int32)
    out = jax.ShapeDtypeStruct((MEMBERS, tile // 2, COLS), jnp.bfloat16)
    heads = pltpu.VMEM((16, tile, COLS), jnp.bfloat16)
    near = pltpu.VMEM((txt + 4 * tile, COLS), jnp.bfloat16)
    return pl.pallas_call(
        layer_kernel,
        out_shape=(out,) * 8,
        in_specs=[SMEM] * 4 + [hbm] * 17 + [VMEM],
        out_specs=(hbm,) * 8,
        scratch_shapes=[
            pltpu.VMEM((4, rows, width), jnp.bfloat16),
            pltpu.VMEM((width, 3 * COLS), jnp.bfloat16),
            pltpu.VMEM((txt, width), jnp.bfloat16),
            heads,
            heads,
            heads,
            near,
            near,
            pltpu.VMEM((8, MEMBERS, tile // 2, COLS), jnp.bfloat16),
            pltpu.SemaphoreType.DMA,
            pltpu.SemaphoreType.DMA((4,)),
            pltpu.SemaphoreType.DMA((4,)),
            pltpu.SemaphoreType.DMA((8,)),
        ],
        compiler_params=pltpu.CompilerParams(vmem_limit_bytes=ROOM),
        cost_estimate=pl.CostEstimate(
            flops=5 * 10**10, bytes_accessed=14 * 2**20, transcendentals=5 * 10**6
        ),
        name="layer",
    )(jnp.concatenate([place, order]), kv_index, kv_count, text_len, *parts, *blocks, *texts, gain)


def pack_kernel(*refs):
    blocks, out, sem = refs[:9], refs[9], refs[10]

    def lay(block, group, slot, to):
        lanes = slice(to * COLS, (to + 1) * COLS)
        pltpu.make_async_copy(block.at[group, :, 3 * COLS :], out.at[slot, :, lanes], sem).start()

    for slot, block in enumerate(blocks[:7]):
        for group in range(4):
            lay(block, group, slot, group)
    for group in range(4):
        lay(blocks[7 + group // 2], group % 2, 7, group)
    pltpu.make_async_copy(out, out, sem).wait()


def pack(blocks):
    _, rows, width = blocks[0].shape
    return pl.pallas_call(
        pack_kernel,
        out_shape=jax.ShapeDtypeStruct((RING, rows, width), jnp.bfloat16),
        in_specs=[pl.BlockSpec(memory_space=pl.ANY)] * 9,
        out_specs=VMEM,
        scratch_shapes=[pltpu.SemaphoreType.DMA],
        compiler_params=pltpu.CompilerParams(vmem_limit_bytes=ROOM),
        cost_estimate=pl.CostEstimate(flops=0, bytes_accessed=2 * 2**20, transcendentals=0),
        name="pack",
    )(*blocks)


def finish_kernel(place, *refs):
    own, others = refs[:8], refs[8:14]
    pieces, refs = refs[14:18], refs[18:]
    acts_from, gate, out, xs, wo, acts, x_sem, wo_sem, acts_sem = refs
    yh, z, core = place[0], place[1], place[2]
    rows = pieces[0].shape[1]
    for other, block in enumerate(pieces):
        for slot, offset in enumerate(RING_ORDER):
            source = lax.rem(z + offset + RING, RING)
            source_yh = flip(yh, other // 2)
            source_core = flip(core, other % 2)
            start = pl.multiple_of((source_yh * 16 + source * 2 + source_core) * rows, 16)
            pltpu.make_async_copy(block.at[slot], wo.at[pl.ds(start, rows)], wo_sem).start()
    for other in range(MEMBERS):
        heads = flip(yh, other // 2) * 2 + flip(core, other % 2)
        lanes = pl.ds(pl.multiple_of(heads * COLS, 128), COLS)
        if other == 0:
            for at in range(8):
                pltpu.make_async_copy(own[at].at[0], xs.at[at, :, lanes], x_sem).start()
        else:
            for part in range(2):
                block = others[part * 3 + other - 1]
                here = slice(part * 4, part * 4 + 4)
                pltpu.make_async_copy(block, xs.at[here, :, lanes], x_sem).start()
    pltpu.make_async_copy(acts_from, acts, acts_sem).start()
    pltpu.make_async_copy(xs, xs, x_sem).wait()
    pltpu.make_async_copy(wo, wo, wo_sem).wait()
    pltpu.make_async_copy(acts_from, acts, acts_sem).wait()
    width = wo.shape[1]
    chunk = width // 3
    for piece in range(3):
        lanes = slice(piece * chunk, (piece + 1) * chunk)
        made = jnp.dot(
            xs[...].reshape(512, width), wo[:, lanes], preferred_element_type=jnp.float32
        )
        for at, distance in enumerate(ORDER):
            sequence = lax.rem(z - distance + RING, RING)
            out[sequence, :, lanes] = (
                acts[sequence, :, lanes].astype(jnp.float32)
                + gate[sequence, :, lanes] * made[at * 64 : (at + 1) * 64]
            ).astype(jnp.bfloat16)


def finish(place, own, others, pieces, acts, gate):
    width = acts.shape[2]
    hbm = pl.BlockSpec(memory_space=pl.ANY)
    return pl.pallas_call(
        finish_kernel,
        out_shape=jax.ShapeDtypeStruct(acts.shape, jnp.bfloat16),
        in_specs=[SMEM] + [hbm] * 19 + [VMEM],
        out_specs=VMEM,
        scratch_shapes=[
            pltpu.VMEM((8, 64, width), jnp.bfloat16),
            pltpu.VMEM((width, width), jnp.bfloat16),
            pltpu.VMEM(acts.shape, jnp.bfloat16),
            pltpu.SemaphoreType.DMA,
            pltpu.SemaphoreType.DMA,
            pltpu.SemaphoreType.DMA,
        ],
        compiler_params=pltpu.CompilerParams(vmem_limit_bytes=ROOM),
        cost_estimate=pl.CostEstimate(
            flops=2 * 512 * 1536 * 1536, bytes_accessed=12 * 2**20, transcendentals=0
        ),
        name="finish",
    )(place, *own, *others, *pieces, acts, gate)


def swap(block, axis):
    return lax.ppermute(block, axis, [(0, 1), (1, 0)])


def toggled(block, axis, bits, size):
    return lax.ppermute(block, axis, [(i, i ^ bits) for i in range(size)])


def moved(block, distance):
    return lax.ppermute(block, "z", [(i, (i + distance) % RING) for i in range(RING)])


def text_rows(text_feat, text_proj):
    section = lax.axis_index("section")
    width = text_proj.shape[1]
    part = jnp.dot(
        text_feat.reshape(-1, text_feat.shape[2]), text_proj, preferred_element_type=jnp.float32
    ).reshape(2, 2, 2, -1, width)
    bits = [(section >> n) & 1 for n in range(3)]
    for n in range(3):
        keep = lax.dynamic_index_in_dim(part, bits[n], 2 - n, keepdims=False)
        send = lax.dynamic_index_in_dim(part, 1 - bits[n], 2 - n, keepdims=False)
        part = keep + toggled(send, "section", 1 << n, SECTIONS)
    rows = unit_rows(part).astype(jnp.bfloat16)
    for n in (2, 1, 0):
        rows = jnp.stack([rows, toggled(rows, "section", 1 << n, SECTIONS)], axis=2 - n)
    for n in range(3):
        rows = jnp.where(bits[n] == 1, jnp.flip(rows, 2 - n), rows)
    return rows.reshape(SECTIONS, -1, width)


def body(acts, attn_proj, modulation, q_gain, text_feat, text_proj, text_len, kv_index, kv_count):
    acts, weights, modulation = acts[0], attn_proj[0], modulation[0]
    sequences, tokens, width = acts.shape
    yh, z, core = (lax.axis_index(name) for name in SEQ)
    member = 2 * yh + core
    place = jnp.stack([yh, z, core]).astype(jnp.int32)

    onward = [(i, (i + 1) % SECTIONS) for i in range(SECTIONS)]
    earlier = lax.ppermute(acts, "section", onward)
    packed = jnp.concatenate([modulation[:, 2], weights[3]])
    packed = lax.ppermute(packed, "section", onward)
    gate = packed[:sequences].astype(jnp.float32)[:, None, :]
    outer = packed[sequences:]

    modulated = modulate(acts, modulation.transpose(1, 0, 2))
    own = lax.all_to_all(modulated, "z", split_axis=0, concat_axis=0, tiled=True)
    own = own.reshape(-1, width)

    mine = []
    for other in range(MEMBERS):
        start = jnp.bitwise_xor(member, other) * COLS
        columns = [lax.dynamic_slice_in_dim(weights[kind], start, COLS, 1) for kind in range(3)]
        columns = jnp.concatenate(columns, axis=1)
        columns = toggled(columns, ("yh", "core"), other, MEMBERS) if other else columns
        mine.append(
            jnp.concatenate([columns, outer[:, other * COLS : (other + 1) * COLS]], axis=1)
        )
    mine = jnp.stack(mine)

    text = text_rows(text_feat, text_proj)
    own, mine = hold([own, mine], [text])
    across, near = swap(own, "yh"), swap(own, "core")
    text = lax.all_to_all(text, "z", split_axis=0, concat_axis=0, tiled=True)
    text = text.reshape(-1, width)
    (mine,) = hold([mine], [own], 10**11)
    right = left = mine
    blocks = [mine]
    for step in range(3):
        right, left = moved(right, 1), moved(left, -1)
        if step == 2:
            right, left = hold([right, left], [text])
        blocks += [right, left]
    right, left = moved(right[:2], 1), moved(left[2:], -1)
    blocks += [right, left]
    (across,) = hold([across], [right, left, earlier])
    far = swap(across, "core")
    text_across = swap(text, "yh")
    texts = (text, swap(text, "core"), text_across, swap(text_across, "core"))

    pieces = pack(blocks)
    pieces_across, pieces_near = swap(pieces, "yh"), swap(pieces, "core")
    gain = lax.dynamic_slice_in_dim(q_gain, member * COLS, COLS, 1)
    parts = (own, near, across, far)
    made = layer(place, kv_index, kv_count, text_len, parts, blocks, texts, gain)
    made = hold(made, [pieces_across, pieces_near])
    pieces = (pieces, pieces_near, pieces_across, swap(pieces_across, "core"))

    def go_home(block, distance):
        route = [
            (s * RING + i, (s + 1) % SECTIONS * RING + (i + distance) % RING)
            for s in range(SECTIONS)
            for i in range(RING)
        ]
        return lax.ppermute(block, ("section", "z"), route)

    def to_swap(blocks):
        return [jnp.stack([one[other] for one in blocks]) for other in range(1, MEMBERS)]

    def exchange(blocks):
        return [
            toggled(block, ("yh", "core"), other + 1, MEMBERS) for other, block in enumerate(blocks)
        ]

    own_heads = [go_home(*one) for one in zip(made, ORDER)]
    other_heads = exchange(to_swap(own_heads[:4])) + exchange(to_swap(own_heads[4:]))
    fresh = finish(place, own_heads, other_heads, pieces, earlier, gate)
    return fresh[None]


def solution(mesh):
    fine = Mesh(mesh.devices.reshape(SECTIONS, 2, RING, 2), ("section",) + SEQ)
    in_specs = (
        P("section", None, SEQ, None),
        P("section", None, SEQ, None),
        P("section", None, None, None),
        P("section", None),
        P(None, SEQ, "section"),
        P("section", None),
        P(),
        P(),
        P(),
    )
    out_specs = P("section", None, SEQ, None)
    return jax.shard_map(body, mesh=fine, in_specs=in_specs, out_specs=out_specs, check_vma=False)
```

```python
import math

import jax
import jax.numpy as jnp
from jax import lax
from jax.experimental import pallas as pl
from jax.experimental.pallas import tpu as pltpu
from jax.sharding import Mesh
from jax.sharding import PartitionSpec as P

HEADS = 12
HEAD_DIM = 128
MEMBERS = 4
PER = HEADS // MEMBERS
COLS = PER * HEAD_DIM
SECTIONS = 8
RING = 8
SEQ = ("yh", "z", "core")
NEG = -1e30
ROOM = 60 * 2**20
VMEM = pl.BlockSpec(memory_space=pltpu.VMEM)
SMEM = pl.BlockSpec(memory_space=pltpu.SMEM)
ORDER = (4, 5, 0, 1, 3, 6, 2, 7)
RING_ORDER = (0, -1, 1, -2, 2, -3, 3, 4)


def unit_rows(values):
    return values * lax.rsqrt(jnp.mean(values * values, axis=-1, keepdims=True) + 1e-06)


def flip(bit, other):
    return bit + other - 2 * bit * other


def modulate_kernel(acts, modulation, out):
    shifts = modulation[0].astype(jnp.float32)
    scales = 1.0 + modulation[1].astype(jnp.float32)
    for at in range(acts.shape[0]):
        inputs = acts[at].astype(jnp.float32)
        mean = jnp.mean(inputs, axis=-1, keepdims=True)
        centred = inputs - mean
        variance = jnp.mean(centred * centred, axis=-1, keepdims=True)
        scaled = centred * lax.rsqrt(variance + 1e-06) * scales[at : at + 1]
        out[at] = (scaled + shifts[at : at + 1]).astype(jnp.bfloat16)


def modulate(acts, modulation):
    return pl.pallas_call(
        modulate_kernel,
        out_shape=jax.ShapeDtypeStruct(acts.shape, acts.dtype),
        in_specs=[VMEM, VMEM],
        out_specs=VMEM,
        compiler_params=pltpu.CompilerParams(vmem_limit_bytes=ROOM),
        cost_estimate=pl.CostEstimate(
            flops=10**11, bytes_accessed=4 * acts.size, transcendentals=0
        ),
        name="modulate",
    )(acts, modulation)


def hold_kernel(*refs):
    del refs


def hold(arrays, earlier=(), flops=0):
    hbm = pl.BlockSpec(memory_space=pl.ANY)
    return pl.pallas_call(
        hold_kernel,
        out_shape=[jax.ShapeDtypeStruct(one.shape, one.dtype) for one in arrays],
        in_specs=[hbm] * (len(arrays) + len(earlier)),
        out_specs=[hbm] * len(arrays),
        input_output_aliases={at: at for at in range(len(arrays))},
        compiler_params=pltpu.CompilerParams(vmem_limit_bytes=ROOM),
        cost_estimate=pl.CostEstimate(flops=flops, bytes_accessed=0, transcendentals=0),
        name="hold",
    )(*arrays, *earlier)


def layer_kernel(place, kv_index, kv_count, text_len, *refs):
    parts, blocks, texts, gain, refs = refs[:4], refs[4:13], refs[13:17], refs[17], refs[18:]
    outs, refs = refs[:8], refs[8:]
    xs, ws, ts, q, k, v, kc, vc, res, w_sem, t_sem, x_sem, out_sem = refs
    yh, z, core = place[0], place[1], place[2]
    rows = blocks[0].shape[1]
    tile, txt = q.shape[1], ts.shape[0]

    def lay(block, members, offset):
        source = lax.rem(z + offset + RING, RING)
        for at, member in enumerate(members):
            source_yh = flip(yh, member // 2)
            source_core = flip(core, member % 2)
            start = pl.multiple_of((source_yh * 16 + source * 2 + source_core) * rows, 16)
            pltpu.make_async_copy(
                block.at[at, :, : 3 * COLS], ws.at[pl.ds(start, rows)], w_sem
            ).start()

    for block, offset in zip(blocks[:7], RING_ORDER):
        lay(block, range(4), offset)
    lay(blocks[7], (0, 1), 4)
    lay(blocks[8], (2, 3), 4)
    quarter = txt // 4
    loads = [pltpu.make_async_copy(one, xs.at[at], x_sem.at[at]) for at, one in enumerate(parts)]
    text_loads = [
        pltpu.make_async_copy(one, ts.at[at * quarter : (at + 1) * quarter], t_sem.at[at])
        for at, one in enumerate(texts)
    ]
    for load in loads + text_loads:
        load.start()
    pltpu.make_async_copy(ws, ws, w_sem).wait()

    for part, load in enumerate(loads):
        load.wait()
        made = jnp.dot(xs[part], ws[...], preferred_element_type=jnp.float32)
        slots = slice(part // 2 * 8, part // 2 * 8 + 8)
        half = slice(part % 2 * (tile // 2), (part % 2 + 1) * (tile // 2))
        for kind, out in enumerate((q, k, v)):
            for head in range(PER):
                lanes = slice(head * HEAD_DIM, (head + 1) * HEAD_DIM)
                first = kind * COLS + head * HEAD_DIM
                mine = made[:, first : first + HEAD_DIM]
                if kind < 2:
                    mine = unit_rows(mine)
                if kind == 0:
                    mine = mine * gain[:, lanes]
                out[slots, half, lanes] = mine.astype(jnp.bfloat16).reshape(
                    8, tile // 2, HEAD_DIM
                )

    for load in text_loads:
        load.wait()
    pair = jnp.dot(ts[...], ws[:, COLS:], preferred_element_type=jnp.float32)
    for head in range(PER):
        lanes = slice(head * HEAD_DIM, (head + 1) * HEAD_DIM)
        kc[:txt, lanes] = unit_rows(pair[:, lanes]).astype(jnp.bfloat16)
    vc[:txt, :] = pair[:, COLS:].astype(jnp.bfloat16)

    scale = math.log2(math.e) / math.sqrt(HEAD_DIM)
    row = lax.broadcasted_iota(jnp.int32, (1, txt), 1)
    row_yh = flip(row // 128, yh)
    row_core = flip((row // 64) % 2, core)
    token = (row_yh * 16 + ((row // 8) % 8) * 2 + row_core) * 8 + row % 8
    bias = jnp.where(token < text_len[z], 0.0, NEG)
    contract = (((1,), (1,)), ((), ()))
    sends = [
        pltpu.make_async_copy(res.at[at], out, out_sem.at[at]) for at, out in enumerate(outs)
    ]

    def one_tile(step, carry):
        at, ry = step // 2, step % 2
        home = lax.rem(z + place[3 + at], RING)
        slot = ry * 8 + home
        index = flip(yh, ry) * 8 + home
        count = kv_count[index]
        for c in range(4):

            @pl.when(c < count)
            def _(c=c):
                near = lax.rem(kv_index[index, c] + 8 * yh, 16)
                here = slice(txt + c * tile, txt + (c + 1) * tile)
                kc[here, :] = k[near]
                vc[here, :] = v[near]

        for n in range(1, 5):

            @pl.when(count == n)
            def _(n=n):
                size = txt + n * tile
                heads = [slice(head * HEAD_DIM, (head + 1) * HEAD_DIM) for head in range(PER)]
                scores = [
                    lax.dot_general(
                        q[slot, :, lanes],
                        kc[:size, lanes],
                        contract,
                        preferred_element_type=jnp.float32,
                    )
                    for lanes in heads
                ]
                scores = [
                    jnp.concatenate([one[:, :txt] * scale + bias, one[:, txt:] * scale], axis=1)
                    for one in scores
                ]
                tops = [jnp.max(one, axis=-1, keepdims=True) for one in scores]
                exps = [jnp.exp2(one - top) for one, top in zip(scores, tops)]
                inverses = [1.0 / jnp.sum(one, axis=-1, keepdims=True) for one in exps]
                probs = [
                    (one * inverse).astype(jnp.bfloat16) for one, inverse in zip(exps, inverses)
                ]
                mixed = [
                    jnp.dot(one, vc[:size, lanes], preferred_element_type=jnp.float32)
                    for one, lanes in zip(probs, heads)
                ]
                for one, lanes in zip(mixed, heads):
                    one = one.astype(jnp.bfloat16)
                    res[at, 2 * ry, :, lanes] = one[: tile // 2]
                    res[at, 2 * ry + 1, :, lanes] = one[tile // 2 :]

        for which, send in enumerate(sends):

            @pl.when(step == 2 * which + 1)
            def _(send=send):
                send.start()

        return carry

    lax.fori_loop(0, 16, one_tile, 0)
    for send in sends:
        send.wait()


def layer(place, kv_index, kv_count, text_len, parts, blocks, texts, gain):
    rows, width = parts[0].shape
    txt = 4 * texts[0].shape[0]
    tile = 128
    hbm = pl.BlockSpec(memory_space=pl.ANY)
    order = jnp.array(ORDER, jnp.int32)
    out = jax.ShapeDtypeStruct((MEMBERS, tile // 2, COLS), jnp.bfloat16)
    heads = pltpu.VMEM((16, tile, COLS), jnp.bfloat16)
    near = pltpu.VMEM((txt + 4 * tile, COLS), jnp.bfloat16)
    return pl.pallas_call(
        layer_kernel,
        out_shape=(out,) * 8,
        in_specs=[SMEM] * 4 + [hbm] * 17 + [VMEM],
        out_specs=(hbm,) * 8,
        scratch_shapes=[
            pltpu.VMEM((4, rows, width), jnp.bfloat16),
            pltpu.VMEM((width, 3 * COLS), jnp.bfloat16),
            pltpu.VMEM((txt, width), jnp.bfloat16),
            heads,
            heads,
            heads,
            near,
            near,
            pltpu.VMEM((8, MEMBERS, tile // 2, COLS), jnp.bfloat16),
            pltpu.SemaphoreType.DMA,
            pltpu.SemaphoreType.DMA((4,)),
            pltpu.SemaphoreType.DMA((4,)),
            pltpu.SemaphoreType.DMA((8,)),
        ],
        compiler_params=pltpu.CompilerParams(vmem_limit_bytes=ROOM),
        cost_estimate=pl.CostEstimate(
            flops=5 * 10**10, bytes_accessed=14 * 2**20, transcendentals=5 * 10**6
        ),
        name="layer",
    )(jnp.concatenate([place, order]), kv_index, kv_count, text_len, *parts, *blocks, *texts, gain)


def pack_kernel(*refs):
    blocks, out, sem = refs[:9], refs[9], refs[10]

    def lay(block, group, slot, to):
        lanes = slice(to * COLS, (to + 1) * COLS)
        pltpu.make_async_copy(block.at[group, :, 3 * COLS :], out.at[slot, :, lanes], sem).start()

    for slot, block in enumerate(blocks[:7]):
        for group in range(4):
            lay(block, group, slot, group)
    for group in range(4):
        lay(blocks[7 + group // 2], group % 2, 7, group)
    pltpu.make_async_copy(out, out, sem).wait()


def pack(blocks):
    _, rows, width = blocks[0].shape
    return pl.pallas_call(
        pack_kernel,
        out_shape=jax.ShapeDtypeStruct((RING, rows, width), jnp.bfloat16),
        in_specs=[pl.BlockSpec(memory_space=pl.ANY)] * 9,
        out_specs=VMEM,
        scratch_shapes=[pltpu.SemaphoreType.DMA],
        compiler_params=pltpu.CompilerParams(vmem_limit_bytes=ROOM),
        cost_estimate=pl.CostEstimate(flops=0, bytes_accessed=2 * 2**20, transcendentals=0),
        name="pack",
    )(*blocks)


def finish_kernel(place, *refs):
    own, others = refs[:8], refs[8:11]
    pieces, refs = refs[11:15], refs[15:]
    acts_from, gate, out, xs, wo, acts, x_sem, wo_sem, acts_sem = refs
    yh, z, core = place[0], place[1], place[2]
    rows = pieces[0].shape[1]
    for other, block in enumerate(pieces):
        for slot, offset in enumerate(RING_ORDER):
            source = lax.rem(z + offset + RING, RING)
            source_yh = flip(yh, other // 2)
            source_core = flip(core, other % 2)
            start = pl.multiple_of((source_yh * 16 + source * 2 + source_core) * rows, 16)
            pltpu.make_async_copy(block.at[slot], wo.at[pl.ds(start, rows)], wo_sem).start()
    for other in range(MEMBERS):
        heads = flip(yh, other // 2) * 2 + flip(core, other % 2)
        lanes = pl.ds(pl.multiple_of(heads * COLS, 128), COLS)
        if other == 0:
            for at in range(8):
                pltpu.make_async_copy(own[at].at[0], xs.at[at, :, lanes], x_sem).start()
        else:
            pltpu.make_async_copy(others[other - 1], xs.at[:, :, lanes], x_sem).start()
    pltpu.make_async_copy(acts_from, acts, acts_sem).start()
    pltpu.make_async_copy(xs, xs, x_sem).wait()
    pltpu.make_async_copy(wo, wo, wo_sem).wait()
    pltpu.make_async_copy(acts_from, acts, acts_sem).wait()
    width = wo.shape[1]
    chunk = width // 3
    for piece in range(3):
        lanes = slice(piece * chunk, (piece + 1) * chunk)
        made = jnp.dot(
            xs[...].reshape(512, width), wo[:, lanes], preferred_element_type=jnp.float32
        )
        for at, distance in enumerate(ORDER):
            sequence = lax.rem(z - distance + RING, RING)
            out[sequence, :, lanes] = (
                acts[sequence, :, lanes].astype(jnp.float32)
                + gate[sequence, :, lanes] * made[at * 64 : (at + 1) * 64]
            ).astype(jnp.bfloat16)


def finish(place, own, others, pieces, acts, gate):
    width = acts.shape[2]
    hbm = pl.BlockSpec(memory_space=pl.ANY)
    return pl.pallas_call(
        finish_kernel,
        out_shape=jax.ShapeDtypeStruct(acts.shape, jnp.bfloat16),
        in_specs=[SMEM] + [hbm] * 16 + [VMEM],
        out_specs=VMEM,
        scratch_shapes=[
            pltpu.VMEM((8, 64, width), jnp.bfloat16),
            pltpu.VMEM((width, width), jnp.bfloat16),
            pltpu.VMEM(acts.shape, jnp.bfloat16),
            pltpu.SemaphoreType.DMA,
            pltpu.SemaphoreType.DMA,
            pltpu.SemaphoreType.DMA,
        ],
        compiler_params=pltpu.CompilerParams(vmem_limit_bytes=ROOM),
        cost_estimate=pl.CostEstimate(
            flops=2 * 512 * 1536 * 1536, bytes_accessed=12 * 2**20, transcendentals=0
        ),
        name="finish",
    )(place, *own, *others, *pieces, acts, gate)


def swap(block, axis):
    return lax.ppermute(block, axis, [(0, 1), (1, 0)])


def toggled(block, axis, bits, size):
    return lax.ppermute(block, axis, [(i, i ^ bits) for i in range(size)])


def moved(block, distance):
    return lax.ppermute(block, "z", [(i, (i + distance) % RING) for i in range(RING)])


def text_rows(text_feat, text_proj):
    section = lax.axis_index("section")
    width = text_proj.shape[1]
    part = jnp.dot(
        text_feat.reshape(-1, text_feat.shape[2]), text_proj, preferred_element_type=jnp.float32
    ).reshape(2, 2, 2, -1, width)
    bits = [(section >> n) & 1 for n in range(3)]
    for n in range(3):
        keep = lax.dynamic_index_in_dim(part, bits[n], 2 - n, keepdims=False)
        send = lax.dynamic_index_in_dim(part, 1 - bits[n], 2 - n, keepdims=False)
        part = keep + toggled(send, "section", 1 << n, SECTIONS)
    rows = unit_rows(part).astype(jnp.bfloat16)
    for n in (2, 1, 0):
        rows = jnp.stack([rows, toggled(rows, "section", 1 << n, SECTIONS)], axis=2 - n)
    for n in range(3):
        rows = jnp.where(bits[n] == 1, jnp.flip(rows, 2 - n), rows)
    return rows.reshape(SECTIONS, -1, width)


def body(acts, attn_proj, modulation, q_gain, text_feat, text_proj, text_len, kv_index, kv_count):
    acts, weights, modulation = acts[0], attn_proj[0], modulation[0]
    sequences, tokens, width = acts.shape
    yh, z, core = (lax.axis_index(name) for name in SEQ)
    member = 2 * yh + core
    place = jnp.stack([yh, z, core]).astype(jnp.int32)

    onward = [(i, (i + 1) % SECTIONS) for i in range(SECTIONS)]
    earlier = lax.ppermute(acts, "section", onward)
    packed = jnp.concatenate([modulation[:, 2], weights[3]])
    packed = lax.ppermute(packed, "section", onward)
    gate = packed[:sequences].astype(jnp.float32)[:, None, :]
    outer = packed[sequences:]

    modulated = modulate(acts, modulation.transpose(1, 0, 2))
    own = lax.all_to_all(modulated, "z", split_axis=0, concat_axis=0, tiled=True)
    own = own.reshape(-1, width)

    mine = []
    for other in range(MEMBERS):
        start = jnp.bitwise_xor(member, other) * COLS
        columns = [lax.dynamic_slice_in_dim(weights[kind], start, COLS, 1) for kind in range(3)]
        columns = jnp.concatenate(columns, axis=1)
        columns = toggled(columns, ("yh", "core"), other, MEMBERS) if other else columns
        mine.append(
            jnp.concatenate([columns, outer[:, other * COLS : (other + 1) * COLS]], axis=1)
        )
    mine = jnp.stack(mine)

    text = text_rows(text_feat, text_proj)
    own, mine = hold([own, mine], [text])
    across, near = swap(own, "yh"), swap(own, "core")
    text = lax.all_to_all(text, "z", split_axis=0, concat_axis=0, tiled=True)
    text = text.reshape(-1, width)
    (mine,) = hold([mine], [own], 10**11)
    right = left = mine
    blocks = [mine]
    for step in range(3):
        right, left = moved(right, 1), moved(left, -1)
        if step == 2:
            right, left = hold([right, left], [text])
        blocks += [right, left]
    right, left = moved(right[:2], 1), moved(left[2:], -1)
    blocks += [right, left]
    pieces = pack(blocks)
    text_across, text_near = swap(text, "yh"), swap(text, "core")
    across, text_across = hold([across, text_across], [right, left, earlier, pieces])
    far = swap(across, "core")
    texts = (text, text_near, text_across, swap(text_across, "core"))
    pieces_across, pieces_near = swap(pieces, "yh"), swap(pieces, "core")
    gain = lax.dynamic_slice_in_dim(q_gain, member * COLS, COLS, 1)
    parts = (own, near, across, far)
    made = layer(place, kv_index, kv_count, text_len, parts, blocks, texts, gain)
    made = hold(made, [pieces_across, pieces_near])
    pieces = (pieces, pieces_near, pieces_across, swap(pieces_across, "core"))

    def go_home(block, distance):
        route = [
            (s * RING + i, (s + 1) % SECTIONS * RING + (i + distance) % RING)
            for s in range(SECTIONS)
            for i in range(RING)
        ]
        return lax.ppermute(block, ("section", "z"), route)

    def to_swap(blocks):
        return [jnp.stack([one[other] for one in blocks]) for other in range(1, MEMBERS)]

    def exchange(blocks):
        return [
            toggled(block, ("yh", "core"), other + 1, MEMBERS) for other, block in enumerate(blocks)
        ]

    own_heads = [go_home(*one) for one in zip(made, ORDER)]
    other_heads = exchange(to_swap(own_heads))
    fresh = finish(place, own_heads, other_heads, pieces, earlier, gate)
    return fresh[None]


def solution(mesh):
    fine = Mesh(mesh.devices.reshape(SECTIONS, 2, RING, 2), ("section",) + SEQ)
    in_specs = (
        P("section", None, SEQ, None),
        P("section", None, SEQ, None),
        P("section", None, None, None),
        P("section", None),
        P(None, SEQ, "section"),
        P("section", None),
        P(),
        P(),
        P(),
    )
    out_specs = P("section", None, SEQ, None)
    return jax.shard_map(body, mesh=fine, in_specs=in_specs, out_specs=out_specs, check_vma=False)
```
